32 devices in a mesh: batch: 8 (over z, x), rows: 4 (over y, core).
Axes of the slice: x: 2, y: 2, z: 4, core: 2. Of those that a mesh axis runs over, the one named last changes fastest.
Arguments:
- inputs: bfloat16 [384, 16, 16, 891], P('batch', 'rows'), may hold values from -14 to 14
- small_flags: int32 [384], P('batch'), may hold values 0 or 1
- norm_params: float32 [2, 1947], replicated, may hold values from -1 to 2.1
- norm_moment: float32 [2, 1947], replicated, may hold values from -384 to 384
- w_bottleneck: float32 [891, 132], replicated, may hold values from -0.1875 to 0.1875
- w_growth: float32 [1188, 33], replicated, may hold values from -0.1875 to 0.1875
- w_transition: float32 [924, 462], replicated, may hold values from -0.1875 to 0.1875
- m_bottleneck: float32 [891, 132], replicated, may hold values from -896 to 896
- m_growth: float32 [1188, 33], replicated, may hold values from -896 to 896
- m_transition: float32 [924, 462], replicated, may hold values from -896 to 896
- cotangent: bfloat16 [384, 8, 8, 462], P(('batch', 'rows')), may hold values from -7 to 7
Outputs:
- pooled: bfloat16 [384, 8, 8, 462], P(('batch', 'rows'))
- input_grad: bfloat16 [384, 16, 16, 891], P('batch', 'rows')
- norm_moment_new: float32 [2, 1947], replicated
- norm_params_new: float32 [2, 1947], replicated
- m_bottleneck_new: float32 [891, 132], replicated
- m_growth_new: float32 [1188, 33], replicated
- m_transition_new: float32 [924, 462], replicated
- w_bottleneck_new: float32 [891, 132], replicated
- w_growth_new: float32 [1188, 33], replicated
- w_transition_new: float32 [924, 462], replicated
The draws below stay inside these ranges and needn't reach their ends.
All inputs are finite; a program needn't handle non-finite values. No bound on the sum of `small_flags` on one device may be relied on, other than what follows from the above.
Results may differ from the reference program's by a relative error of at most 0.0089.
Values may be sent and summed in bfloat16 or wider, within the bound.
A program may use at most 192 MiB of HBM per device.

```python
import jax
import jax.numpy as jnp
from jax import lax

C0 = 891
BOT = 132
GR = 33
TRANS = 462
SIDE = 16
SMALL = 12
NS_STEPS = 5
IMG_DEV = 48
IMAGES = 384
CAT = 924


def rising(item_count, top_value):
    place = jnp.arange(item_count, dtype=jnp.float32) / (item_count - 1)
    return jnp.sqrt(1.0 + top_value * place)


def moment_like(key, row_total, col_total, factor):
    spread = factor * jnp.sqrt(221.0 * IMAGES)
    return spread * jax.random.truncated_normal(key, -4.0, 4.0, (row_total, col_total), jnp.float32)


def draw_inputs(key, part):
    key = jax.random.fold_in(key, 11)
    noise_key, offset_key = jax.random.split(key)
    shape_all = (IMAGES, SIDE, SIDE, C0)
    noise = jax.random.truncated_normal(noise_key, -4.0, 4.0, shape_all, jnp.float32)
    image_scale = rising(IMAGES, 2.0)
    offset = 0.5 * jax.random.uniform(offset_key, (C0,), jnp.float32, -1.0, 1.0)
    row_scale = rising(SIDE, 2.0)
    values = image_scale[:, None, None, None] * row_scale[None, :, None, None] * (noise + offset)
    return values.astype(jnp.bfloat16)


def draw_norm_params(key, part):
    key = jax.random.fold_in(key, 12)
    spread_key, shift_key = jax.random.split(key)
    total = C0 + BOT + C0 + GR
    ramp = jnp.concatenate([rising(C0, 2.0), rising(BOT, 2.0), rising(C0 + GR, 2.0)])
    gains = ramp * jax.random.uniform(spread_key, (total,), jnp.float32, 0.8, 1.2)
    shifts = 0.3 * jax.random.truncated_normal(shift_key, -3.0, 3.0, (total,), jnp.float32)
    return jnp.stack([gains, shifts])


def draw_norm_moment(key, part):
    key = jax.random.fold_in(key, 13)
    return moment_like(key, 2, C0 + BOT + C0 + GR, 0.02)


def draw_m_bottleneck(key, part):
    key = jax.random.fold_in(key, 14)
    return moment_like(key, C0, BOT, 0.1)


def draw_m_growth(key, part):
    key = jax.random.fold_in(key, 15)
    return moment_like(key, 9 * BOT, GR, 0.24)


def draw_m_transition(key, part):
    key = jax.random.fold_in(key, 16)
    return moment_like(key, C0 + GR, TRANS, 0.33)


def draw_cotangent(key, part):
    key = jax.random.fold_in(key, 17)
    shape_all = (IMAGES, SIDE // 2, SIDE // 2, TRANS)
    noise = jax.random.truncated_normal(key, -4.0, 4.0, shape_all, jnp.float32)
    image_scale = rising(IMAGES, 2.0)
    return (image_scale[:, None, None, None] * noise).astype(jnp.bfloat16)


def place_ends(array, stream_key, least, high):
    longest = array.shape.index(max(array.shape))
    spots = []
    for shift in (0, 1):
        where = [jax.random.randint(jax.random.fold_in(stream_key, axis), (), 0, length) for axis, length in enumerate(array.shape)]
        where[longest] = (where[longest] + shift) % array.shape[longest]
        spots.append(tuple(where))
    return array.at[spots[0]].set(least).at[spots[1]].set(high)


def centred(key, extent, deviation, bound, held_as=jnp.bfloat16):
    result = deviation * jax.random.normal(key, extent, jnp.float32)
    return jnp.clip(result, min=-bound, max=bound).astype(held_as)


def setup_inputs(seed: int = 0) -> dict:
    key_list = jax.random.split(jax.random.key(seed), 12)
    return {
        "inputs": draw_inputs(jax.random.fold_in(key_list[11], 71), 0),
        "small_flags": place_ends((jax.random.randint(key_list[1], (IMAGES,), 0, 16) < 5).astype(jnp.int32), jax.random.fold_in(key_list[1], 1), 0, 1),
        "norm_params": draw_norm_params(jax.random.fold_in(key_list[11], 71), 0),
        "norm_moment": draw_norm_moment(jax.random.fold_in(key_list[11], 71), 0),
        "w_bottleneck": centred(key_list[4], (C0, BOT), C0 ** -0.5, 0.1875, jnp.float32),
        "w_growth": centred(key_list[5], (9 * BOT, GR), (9 * BOT) ** -0.5, 0.1875, jnp.float32),
        "w_transition": centred(key_list[6], (CAT, TRANS), CAT ** -0.5, 0.1875, jnp.float32),
        "m_bottleneck": draw_m_bottleneck(jax.random.fold_in(key_list[11], 71), 0),
        "m_growth": draw_m_growth(jax.random.fold_in(key_list[11], 71), 0),
        "m_transition": draw_m_transition(jax.random.fold_in(key_list[11], 71), 0),
        "cotangent": draw_cotangent(jax.random.fold_in(key_list[11], 71), 0),
    }


@jax.custom_vjp
def low(v):
    return lax.optimization_barrier(v.astype(jnp.bfloat16)).astype(jnp.float32)

@jax.custom_vjp
def low_back(v):
    return v

def low_keep(v):
    return (low(v), None)

def low_pass(kept, grad):
    return (grad,)

def back_keep(v):
    return (v, None)

def back_low(kept, grad):
    return (low(grad),)
low.defvjp(low_keep, low_pass)
low_back.defvjp(back_keep, back_low)
EPSILON = 1e-05
MOMENTUM_DECAY = 0.9
MUON_RATE = 0.5
NORM_RATE = 1.0
QUINTIC_A = 3.4445
QUINTIC_B = -4.775
QUINTIC_C = 2.0315
TINY = 1e-07
PRECISE = lax.Precision.HIGHEST

def valid_cells(small_flags):
    row_ids = lax.broadcasted_iota(jnp.int32, (SIDE, SIDE), 0)
    col_ids = lax.broadcasted_iota(jnp.int32, (SIDE, SIDE), 1)
    inside = jnp.where((row_ids < SMALL) & (col_ids < SMALL), 1.0, 0.0).astype(jnp.float32)
    is_small = (small_flags > 0)[:, None, None]
    return jnp.where(is_small, inside[None], jnp.ones_like(inside)[None])

def channel_sums(values, mask_cells):
    weighted = values * mask_cells[..., None]
    return (lax.optimization_barrier(jnp.sum(weighted, axis=(0, 1, 2))), lax.optimization_barrier(jnp.sum(weighted * values, axis=(0, 1, 2))))

def normalize(values, total_sum, total_square, cell_count):
    mean_value = total_sum / cell_count
    inverse = lax.rsqrt(total_square / cell_count - mean_value * mean_value + EPSILON)
    return (values - mean_value) * inverse

def image_taps(values):
    images_here, map_height, map_width, channels = values.shape
    padded = jnp.pad(values, ((0, 0), (1, 1), (1, 1), (0, 0)))
    pieces = [padded[:, tap_row:tap_row + map_height, tap_col:tap_col + map_width, :] for tap_row in range(3) for tap_col in range(3)]
    return jnp.stack(pieces, axis=-1).reshape(images_here, map_height, map_width, channels * 9)

def forward_pass(features, w_first, w_taps, w_last, params, mask_cells):
    block_count = IMAGES // IMG_DEV
    block_shape = (block_count, IMG_DEV, SIDE, SIDE)
    cell_count = jnp.sum(mask_cells)
    all_gains = params[0]
    all_shifts = params[1]
    gain_first = all_gains[:C0]
    shift_first = all_shifts[:C0]
    gain_middle = all_gains[C0:C0 + BOT]
    shift_middle = all_shifts[C0:C0 + BOT]
    gain_last = all_gains[C0 + BOT:]
    shift_last = all_shifts[C0 + BOT:]
    low_first = low(w_first)
    low_taps = low(w_taps)
    low_last = low(w_last)
    feature_blocks = features.reshape(block_shape + (C0,))
    mask_blocks = mask_cells.reshape(block_shape)
    first_parts = lax.map(jax.checkpoint(lambda pair: channel_sums(pair[0], pair[1])), (feature_blocks, mask_blocks))
    first_sum = lax.optimization_barrier(jnp.sum(first_parts[0], axis=0))
    first_square = lax.optimization_barrier(jnp.sum(first_parts[1], axis=0))

    def first_section(pair):
        first_hat = normalize(pair[0], first_sum, first_square, cell_count)
        first_act = low(jax.nn.silu(first_hat * gain_first + shift_first) * pair[1][..., None])
        return low_back(jnp.dot(first_act, low_first, precision=PRECISE, preferred_element_type=jnp.float32))
    bottleneck = lax.map(jax.checkpoint(first_section), (feature_blocks, mask_blocks))
    middle_sum, middle_square = channel_sums(bottleneck.reshape((IMAGES, SIDE, SIDE, BOT)), mask_cells)

    def middle_section(pair):
        middle_hat = normalize(pair[0], middle_sum, middle_square, cell_count)
        middle_act = low(jax.nn.silu(middle_hat * gain_middle + shift_middle) * pair[1][..., None])
        return low_back(jnp.dot(image_taps(middle_act), low_taps, precision=PRECISE, preferred_element_type=jnp.float32))
    growth = lax.map(jax.checkpoint(middle_section), (bottleneck, mask_blocks))
    growth_sum, growth_square = channel_sums(growth.reshape((IMAGES, SIDE, SIDE, GR)), mask_cells)
    last_sum = jnp.concatenate([first_sum, growth_sum])
    last_square = jnp.concatenate([first_square, growth_square])

    def last_section(triple):
        joined = jnp.concatenate([triple[0], triple[1]], axis=-1)
        last_hat = normalize(joined, last_sum, last_square, cell_count)
        transition_in = low((last_hat * gain_last + shift_last) * triple[2][..., None])
        transition = low_back(jnp.dot(transition_in, low_last, precision=PRECISE, preferred_element_type=jnp.float32))
        grouped = transition.reshape(IMG_DEV, SIDE // 2, 2, SIDE // 2, 2, TRANS)
        return 0.25 * lax.optimization_barrier(jnp.sum(grouped, axis=(2, 4)))
    pooled = lax.map(jax.checkpoint(last_section), (feature_blocks, growth, mask_blocks))
    return pooled.reshape(IMAGES, SIDE // 2, SIDE // 2, TRANS)

def orthogonal(moment):
    current = moment / (jnp.sqrt(jnp.sum(moment * moment)) + TINY)
    for sweep_index in range(NS_STEPS):
        gram_part = jnp.dot(current.T, current, precision=PRECISE)
        poly_part = QUINTIC_B * gram_part + QUINTIC_C * jnp.dot(gram_part, gram_part, precision=PRECISE)
        current = QUINTIC_A * current + jnp.dot(current, poly_part, precision=PRECISE)
    return current

def reference(inputs, small_flags, norm_params, norm_moment, w_bottleneck, w_growth, w_transition, m_bottleneck, m_growth, m_transition, cotangent):
    mask_cells = valid_cells(small_flags)
    cell_count = jnp.sum(mask_cells)
    features = inputs.astype(jnp.float32)

    def wrapped(feature_values, w_first, w_taps, w_last, params):
        return forward_pass(feature_values, w_first, w_taps, w_last, params, mask_cells)
    pooled, pullback = jax.vjp(wrapped, features, w_bottleneck, w_growth, w_transition, norm_params)
    grad_input, grad_first, grad_taps, grad_last, grad_params = pullback(cotangent.astype(jnp.float32))
    norm_moment_new = MOMENTUM_DECAY * norm_moment + grad_params
    norm_params_new = norm_params - NORM_RATE * norm_moment_new / jnp.sqrt(cell_count)
    m_first_new = MOMENTUM_DECAY * m_bottleneck + grad_first
    m_taps_new = MOMENTUM_DECAY * m_growth + grad_taps
    m_last_new = MOMENTUM_DECAY * m_transition + grad_last
    w_first_new = w_bottleneck - MUON_RATE * orthogonal(m_first_new)
    w_taps_new = w_growth - MUON_RATE * orthogonal(m_taps_new)
    w_last_new = w_transition - MUON_RATE * orthogonal(m_last_new)
    return (pooled.astype(jnp.bfloat16), grad_input.astype(jnp.bfloat16), norm_moment_new, norm_params_new, m_first_new, m_taps_new, m_last_new, w_first_new, w_taps_new, w_last_new)
```

```python
import functools

import jax
import jax.numpy as jnp
from jax import lax
from jax.experimental import pallas as pl
from jax.experimental.pallas import tpu as pltpu
from jax.sharding import PartitionSpec as P

SMALL = 12
NS_STEPS = 5
EPSILON = 1e-05
MOMENTUM_DECAY = 0.9
MUON_RATE = 0.5
NORM_RATE = 1.0
QUINTIC_A = 3.4445
QUINTIC_B = -4.775
QUINTIC_C = 2.0315
TINY = 1e-07
F32 = jnp.float32
BF16 = jnp.bfloat16
MESH = pl.DeviceIdType.MESH
LANES = 128
TILE_IMGS = 4
VMEM_BYTES = 62 * 1024 * 1024


def dot(a, b, ca, cb):
    return lax.dot_general(a, b, (((ca,), (cb,)), ((), ())), preferred_element_type=F32)


def split(a):
    high = a.astype(BF16)
    return high, (a - high.astype(F32)).astype(BF16)


def round_up(value, step):
    return -(-value // step) * step


def fold_rows(value):
    rows, cols = value.shape
    return jnp.sum(value.reshape(rows // 8, 8, cols), axis=0)


def lane_tiles(total):
    return [(j, min(LANES, total - j)) for j in range(0, total, LANES)]


def lane_blocks(total):
    return [(j, min(2 * LANES, total - j)) for j in range(0, total, 2 * LANES)]


def zeros_for(pieces):
    return tuple(jnp.zeros((8, w), F32) for _, w in pieces)


def pack_row(slots, r, top, row):
    for k, (j, w) in enumerate(lane_tiles(row.shape[1])):
        slots[r, top + k : top + k + 1, 0:w] = row[:, j : j + w]


def unpack_row(total, top, size):
    return jnp.concatenate([total[top + k : top + k + 1, 0:w] for k, (_, w) in enumerate(lane_tiles(size))], axis=1)


def row_sum(value):
    return jnp.sum(value, axis=0, keepdims=True)


class VectorReduce:
    def __init__(self, place, counts, refs):
        self.r, self.b = place
        self.rows, self.batch = counts
        self.row_slots, self.batch_slots, self.row_sems, self.batch_sems = refs

    def copies(self, axis, me, count, slots, sems):
        made = []
        for step in range(1, count):
            peer = lax.rem(me + step, count)
            made.append(
                pltpu.make_async_remote_copy(
                    src_ref=slots.at[me],
                    dst_ref=slots.at[me],
                    send_sem=sems.at[0, step],
                    recv_sem=sems.at[1, step],
                    device_id={axis: peer},
                    device_id_type=MESH,
                )
            )
        return made

    def start(self):
        self.first = self.copies("rows", self.r, self.rows, self.row_slots, self.row_sems)
        for copy in self.first:
            copy.start()

    def middle(self):
        for copy in self.first:
            copy.wait_recv()
        total = self.row_slots[0]
        for j in range(1, self.rows):
            total = total + self.row_slots[j]
        self.batch_slots[self.b] = total
        self.second = self.copies("batch", self.b, self.batch, self.batch_slots, self.batch_sems)
        for copy in self.second:
            copy.start()

    def finish(self):
        for copy in self.second:
            copy.wait_recv()
        total = self.batch_slots[0]
        for j in range(1, self.batch):
            total = total + self.batch_slots[j]
        for copy in self.first + self.second:
            copy.wait_send()
        return total


class BlockReduce:
    def __init__(self, place, counts, refs):
        self.r, self.b = place
        self.batch = counts[1]
        self.local, self.out_a, self.in_a, self.in_b, self.in_c, self.full, self.sems = refs
        self.length = self.local.shape[0]
        self.out_b = self.out_a.at[pl.ds(0, self.length // 4)]
        self.out_c = self.out_a.at[pl.ds(self.length // 4, self.length // 4)]
        self.chunk = self.length // (4 * self.batch)
        self.low, self.high = lax.rem(self.r, 2), lax.div(self.r, 2)
        self.near = self.r + 1 - 2 * self.low
        self.far = self.r + 2 - 4 * self.high

    def each(self, count, body):
        step = 16
        for size in (256, 128, 64, 32):
            if count % size == 0:
                step = size
                break

        def run(i, carry):
            body(pl.multiple_of(i * step, 16), step)
            return carry

        lax.fori_loop(0, count // step, run, 0)

    def copy(self, src, dst, axis, peer, slot):
        return pltpu.make_async_remote_copy(
            src_ref=src,
            dst_ref=dst,
            send_sem=self.sems.at[0, slot],
            recv_sem=self.sems.at[1, slot],
            device_id={axis: peer},
            device_id_type=MESH,
        )

    def at(self, start, size):
        return pl.ds(pl.multiple_of(start, 16), size)

    def start(self):
        half = self.length // 2
        other = (1 - self.low) * half

        def body(i, n):
            self.out_a[self.at(i, n)] = self.local[self.at(other + i, n)].astype(BF16)

        self.each(half, body)
        self.a = self.copy(self.out_a, self.in_a, "rows", self.near, 0)
        self.a.start()

    def step_b(self):
        quarter = self.length // 4
        self.a.wait()
        other = (1 - self.high) * quarter
        mine = self.low * 2 * quarter

        def body(i, n):
            total = self.local[self.at(mine + other + i, n)] + self.in_a[self.at(other + i, n)].astype(F32)
            self.out_b[self.at(i, n)] = total.astype(BF16)

        self.each(quarter, body)
        self.b_copy = self.copy(self.out_b, self.in_b, "rows", self.far, 1)
        self.b_copy.start()

    def step_c(self):
        quarter = self.length // 4
        self.b_copy.wait()
        mine = self.low * 2 * quarter + self.high * quarter

        def body(i, n):
            total = self.local[self.at(mine + i, n)] + self.in_a[self.at(self.high * quarter + i, n)].astype(F32)
            total = total + self.in_b[self.at(i, n)].astype(F32)
            self.local[self.at(mine + i, n)] = total
            self.out_c[self.at(i, n)] = total.astype(BF16)

        self.each(quarter, body)
        self.c = []
        for step in range(1, self.batch):
            peer = lax.rem(self.b + step, self.batch)
            piece = self.out_c.at[self.at(peer * self.chunk, self.chunk)]
            self.c.append(self.copy(piece, self.in_c.at[step], "batch", peer, 1 + step))
        for copy in self.c:
            copy.start()

    def step_d(self):
        quarter = self.length // 4
        for copy in self.c:
            copy.wait()
        mine = self.low * 2 * quarter + self.high * quarter + self.b * self.chunk

        def body(i, n):
            total = self.local[self.at(mine + i, n)]
            for step in range(1, self.batch):
                total = total + self.in_c[step, self.at(i, n)].astype(F32)
            self.full[self.at(mine + i, n)] = total.astype(BF16)

        self.each(self.chunk, body)
        piece = self.full.at[self.at(mine, self.chunk)]
        self.d = []
        for step in range(1, self.batch):
            peer = lax.rem(self.b + step, self.batch)
            self.d.append(self.copy(piece, piece, "batch", peer, self.batch + step))
        for copy in self.d:
            copy.start()

    def step_e(self):
        quarter = self.length // 4
        for copy in self.d:
            copy.wait()
        self.e_copy().start()

    def e_copy(self):
        quarter = self.length // 4
        piece = self.full.at[self.at(self.low * 2 * quarter + self.high * quarter, quarter)]
        return self.copy(piece, piece, "rows", self.far, 2 * self.batch)

    def step_f(self):
        half = self.length // 2
        self.e_copy().wait()
        piece = self.full.at[self.at(self.low * half, half)]
        self.f = self.copy(piece, piece, "rows", self.near, 2 * self.batch + 1)
        self.f.start()

    def finish(self):
        self.f.wait()

    @staticmethod
    def scratch(length, batch):
        shapes = (length // 2, length // 2, length // 4)
        return (
            [pltpu.VMEM((length, LANES), F32)]
            + [pltpu.VMEM((n, LANES), BF16) for n in shapes]
            + [
                pltpu.VMEM((batch, length // (4 * batch), LANES), BF16),
                pltpu.VMEM((length, LANES), BF16),
                pltpu.SemaphoreType.DMA((2, 2 * batch + 2)),
            ]
        )


def band_kernel(dims, flags, x_hbm, cot_hbm, params, wf_hbm, wg_hbm, wl_hbm, *rest):
    (rows, batch, images, c0, bot, gr, trans, own) = dims
    cat = c0 + gr
    (ig_hbm, pool_hbm, stats, sum_a, sum_c) = rest[:5]
    rest = list(rest[5:])

    def take(n):
        taken = rest[:n]
        del rest[:n]
        return taken

    (xv, av, sv, mv, pmv, px, tin, ting, ev, eg, cotv) = take(11)
    (bnv, a2v, s2v, gv, ggv, gmv) = take(6)
    (wlf, wlb, wlg, wff, wfb, wfn, wgf, wft, wfm, wbm, pmat, umat, cvec, poolv, gt) = take(15)
    (x_sems, io_sems, cot_sems, halo_sems, gg_sems, pool_sems) = take(6)
    small = [take(4) for _ in range(4)]
    small.append(small[0][:2] + take(2))
    small.append(take(4))
    big = [take(7) for _ in range(2)]
    up = take(1)[0]
    local_b = local_c = big[1][0]

    r, b = lax.axis_index("rows"), lax.axis_index("batch")
    place, counts = (r, b), (rows, batch)
    n_pix, n_cell = images * 64, images * 16
    tiles = images // TILE_IMGS
    tp, tc = TILE_IMGS * 64, TILE_IMGS * 16

    w_copies = [
        pltpu.make_async_copy(wf_hbm, wff, io_sems.at[0]),
        pltpu.make_async_copy(wg_hbm, wgf, io_sems.at[1]),
        pltpu.make_async_copy(wl_hbm, wlf, io_sems.at[2]),
    ]
    w_copies[1].start()
    x_copies = [
        pltpu.make_async_copy(x_hbm.at[pl.ds(pl.multiple_of(t * tp, tp), tp)], xv.at[pl.ds(pl.multiple_of(t * tp, tp), tp)], x_sems.at[t]) for t in range(tiles)
    ]
    for copy in x_copies:
        copy.start()
    w_copies[0].start()
    w_copies[2].start()
    cot_own = pltpu.make_async_copy(
        cot_hbm.at[:, pl.ds(pl.multiple_of(r * 16, 16), 16)], cotv.at[pl.ds(r * own, own)], io_sems.at[3]
    )
    cot_own.start()
    barrier = pltpu.get_barrier_semaphore()
    for axis, me, count in (("rows", r, rows), ("batch", b, batch)):
        for step in range(1, count):
            pl.semaphore_signal(barrier, inc=1, device_id={axis: lax.rem(me + step, count)}, device_id_type=MESH)

    a_id = lax.broadcasted_iota(jnp.int32, (tc, tp), 0)
    b_id = lax.broadcasted_iota(jnp.int32, (tc, tp), 1)
    hit = (a_id // 8 == b_id // 32) & (a_id % 8 == (b_id % 16) // 2)
    pmat[...] = jnp.where(hit, 1.0, 0.0).astype(BF16)
    a_id = lax.broadcasted_iota(jnp.int32, (tp, tc), 1)
    b_id = lax.broadcasted_iota(jnp.int32, (tp, tc), 0)
    hit = (a_id // 8 == b_id // 32) & (a_id % 8 == (b_id % 16) // 2)
    umat[...] = jnp.where(hit, 1.0, 0.0).astype(BF16)

    pix = lax.broadcasted_iota(jnp.int32, (64, 1), 0)
    inside = jnp.where((r * 4 + pix // 16 < SMALL) & (pix % 16 < SMALL), 1.0, 0.0)
    cell = lax.broadcasted_iota(jnp.int32, (16, 1), 0)
    inside_cell = jnp.where((r * 4 + cell // 8 * 2 < SMALL) & (cell % 8 * 2 < SMALL), 1.0, 0.0)
    inside_above = jnp.where((r * 4 - 1 < SMALL) & (cell < SMALL), 1.0, 0.0)
    inside_below = jnp.where((r * 4 + 4 < SMALL) & (cell < SMALL), 1.0, 0.0)
    have_above = jnp.where(r > 0, 1.0, 0.0)
    have_below = jnp.where(r < rows - 1, 1.0, 0.0)
    inside_count = jnp.clip(SMALL - r * 4, 0, 4) * SMALL

    copy_id = lax.broadcasted_iota(jnp.int32, (LANES, gr), 0)
    lane_id = lax.broadcasted_iota(jnp.int32, (LANES, gr), 1)
    spread = jnp.where((copy_id % gr == lane_id) & (copy_id < 3 * gr), 1.0, 0.0).astype(BF16)
    w_copies[1].wait()
    wgb = wgf[...].astype(BF16)
    gap = lax.broadcasted_iota(jnp.int32, (9 * bot, bot), 0) - 9 * lax.broadcasted_iota(jnp.int32, (9 * bot, bot), 1)
    wft[...] = jnp.zeros_like(wft)
    for dh in range(3):
        for dw in range(3):
            pick = jnp.where(gap == 3 * dh + dw, 1.0, 0.0).astype(BF16)
            tap = dot(wgb, pick, 1, 0)
            for c in range(3):
                wft[dh, LANES * dw + gr * c : LANES * dw + gr * (c + 1), :] = tap
            wft[3, LANES * dw + gr * dh : LANES * dw + gr * (dh + 1), :] = tap
    for dh in range(3):
        wfm[dh] = wft[dh].T.astype(BF16)
    wbm[...] = wft[3].astype(BF16)


    tiles_c0, blocks_c0 = lane_tiles(c0), lane_blocks(c0)

    def sums_body(t, carry):
        acc, acc2, count = carry
        pltpu.make_async_copy(x_hbm.at[pl.ds(pl.multiple_of(t * tp, tp), tp)], xv.at[pl.ds(pl.multiple_of(t * tp, tp), tp)], x_sems.at[t]).wait()
        for q in range(TILE_IMGS):
            img = t * TILE_IMGS + q
            is_small = flags[img] > 0
            count = count + jnp.where(is_small, inside_count, 64)
            mask = jnp.where(is_small, inside, 1.0)
            mv[pl.ds(img * 64, 64), :] = jnp.broadcast_to(mask, (64, LANES))
            pmv[pl.ds(img * 16, 16), :] = jnp.broadcast_to(jnp.where(is_small, inside_cell, 1.0), (16, LANES))
        squares, firsts = [], []
        for k, (j, w) in enumerate(tiles_c0):
            total = acc2[k]
            for i in range(0, tp, 32):
                x = xv[pl.ds(pl.multiple_of(t * tp + i, 32), 32), j : j + w].astype(F32)
                total = total + fold_rows(x * x * mv[pl.ds(pl.multiple_of(t * tp + i, 32), 32), 0:w])
            squares.append(total)
        for k, (j, w) in enumerate(blocks_c0):
            cells = dot(pmat[...], xv[pl.ds(pl.multiple_of(t * tp, tp), tp), j : j + w], 1, 0) * pmv[pl.ds(pl.multiple_of(t * tc, tc), tc), 0:1]
            px[pl.ds(pl.multiple_of(t * tc, tc), tc), j : j + w] = cells
            firsts.append(acc[k] + fold_rows(cells))
        return tuple(firsts), tuple(squares), count

    acc, acc2, count = lax.fori_loop(0, tiles, sums_body, (zeros_for(blocks_c0), zeros_for(tiles_c0), jnp.int32(0)))
    acc, acc2 = jnp.concatenate(acc, axis=1), jnp.concatenate(acc2, axis=1)
    red1 = VectorReduce(place, counts, small[0])
    slot = small[0][0]
    span = len(tiles_c0)
    pack_row(slot, r, 0, row_sum(acc))
    pack_row(slot, r, span, row_sum(acc2))
    slot[r, 2 * span : 2 * span + 1, :] = jnp.full((1, LANES), count.astype(F32))
    pl.semaphore_wait(barrier, rows - 1 + batch - 1)
    red1.start()

    w_copies[0].wait()
    w_copies[2].wait()
    wfb[...] = wff[...].astype(BF16)
    wfn[...] = wff[...].T.astype(BF16)
    wlb[...] = wlf[...].astype(BF16)
    red1.middle()
    cot_copies = []
    for step in range(1, rows):
        peer = lax.rem(r + step, rows)
        cot_copies.append(
            pltpu.make_async_remote_copy(
                src_ref=cot_hbm.at[:, pl.ds(pl.multiple_of(peer * 16, 16), 16)],
                dst_ref=cotv.at[pl.ds(r * own, own)],
                send_sem=cot_sems.at[0, step],
                recv_sem=cot_sems.at[1, step],
                device_id={"rows": peer},
                device_id_type=MESH,
            )
        )
    for copy in cot_copies:
        copy.start()

    wlg[...] = dot(spread, wlf[c0:cat, :].astype(BF16), 1, 0).astype(BF16)
    total = red1.finish()
    count_all = total[2 * span : 2 * span + 1, 0:1]
    per = 1.0 / count_all
    mean1 = unpack_row(total, 0, c0) * per
    inv1 = lax.rsqrt(unpack_row(total, span, c0) * per - mean1 * mean1 + EPSILON)
    gain1, shift1 = params[0:1, 0:c0], params[1:2, 0:c0]
    gain2, shift2 = params[0:1, c0 : c0 + bot], params[1:2, c0 : c0 + bot]
    gain3, shift3 = params[0:1, c0 + bot : 2 * c0 + bot], params[1:2, c0 + bot : 2 * c0 + bot]
    gaing, shiftg = params[0:1, 2 * c0 + bot :], params[1:2, 2 * c0 + bot :]
    half_a = 0.5 * gain1 * inv1
    half_b = 0.5 * shift1 - mean1 * half_a
    trans_a = gain3 * inv1
    trans_b = shift3 - mean1 * trans_a
    cvec[0:1, 0:c0] = half_a
    cvec[1:2, 0:c0] = half_b
    cvec[2:3, 0:c0] = 0.25 * trans_a
    cvec[3:4, 0:c0] = trans_b
    cvec[4:5, 0:c0] = mean1
    cvec[5:6, 0:c0] = inv1
    cvec[6:7, 0:c0] = gain1 * inv1
    cvec[7:8, 0:c0] = trans_a

    def first_act(t):
        for j, w in tiles_c0:
            cols = slice(j, j + w)
            scale, shift = cvec[0:1, cols], cvec[1:2, cols]
            for i in range(0, tp, 32):
                at = pl.ds(pl.multiple_of(t * tp + i, 32), 32)
                h = xv[at, cols].astype(F32) * scale + shift
                th = jnp.tanh(h)
                ht = h * th
                av[at, cols] = (h + ht).astype(BF16)
                sv[at, cols] = ((1.0 + th) * (1.0 + (h - ht))).astype(BF16)
            scale, shift = cvec[2:3, cols], cvec[3:4, cols]
            for i in range(0, tc, 32):
                ct = pl.ds(pl.multiple_of(t * tc + i, 32), 32)
                tin[ct, cols] = (px[ct, cols] * scale + pmv[ct, 0:w] * shift).astype(BF16)

    def first_product(t, carry):
        acc, acc2 = carry
        at = pl.ds(pl.multiple_of(t * tp, tp), tp)
        value = dot(av[at, :], wfn[...], 1, 0) * mv[at, 0:1]
        bnv[pl.ds(t * TILE_IMGS, TILE_IMGS)] = value.reshape(TILE_IMGS, 4, 16, bot)
        return acc + fold_rows(value), acc2 + fold_rows(value * value)

    def first_body(t, carry):
        carry = first_product(t - 1, carry)
        first_act(t)
        return carry

    zero = jnp.zeros((8, bot), F32)
    first_act(0)
    acc, acc2 = first_product(tiles - 1, lax.fori_loop(1, tiles, first_body, (zero, zero)))
    red2 = VectorReduce(place, counts, small[1])
    slot = small[1][0]
    pack_row(slot, r, 0, row_sum(acc))
    pack_row(slot, r, 2, row_sum(acc2))
    red2.start()
    a2v[:, 1] = bnv[:, 0].astype(BF16)
    a2v[:, 4] = bnv[:, 3].astype(BF16)

    def edge_copy(ref, sems, side, send):
        return pltpu.make_async_remote_copy(
            src_ref=ref.at[:, 1 + 3 * side],
            dst_ref=ref.at[:, 5 - 5 * side if send else 5 * side],
            send_sem=sems.at[0, side],
            recv_sem=sems.at[1, 1 - side if send else side],
            device_id={"rows": lax.rem(r + rows - 1 + 2 * side, rows)},
            device_id_type=MESH,
        )

    def on_edges(action):
        pl.when(r > 0)(lambda: action(0))
        pl.when(r < rows - 1)(lambda: action(1))

    on_edges(lambda side: edge_copy(a2v, halo_sems, side, True).start())
    cot_own.wait()
    for copy in cot_copies:
        copy.wait()
    red2.middle()

    cot_all = cotv[...].reshape(n_cell, trans)
    eg[...] = dot(cot_all, wlg[...], 1, 1)
    acc_e, acc_ex = [], []
    for j, w in blocks_c0:
        value = dot(cot_all, wlb[j : j + w, :], 1, 1)
        ev[:, j : j + w] = value
        total, total2 = jnp.zeros((8, w), F32), jnp.zeros((8, w), F32)
        for i in range(0, n_cell, 32):
            piece = value[i : i + 32]
            total = total + fold_rows(piece * pmv[i : i + 32, 0:1])
            total2 = total2 + fold_rows(piece * px[i : i + 32, j : j + w])
        acc_e.append(total)
        acc_ex.append(total2)
    acc_e, acc_ex = jnp.concatenate(acc_e, axis=1), jnp.concatenate(acc_ex, axis=1)
    red6 = VectorReduce(place, counts, small[5])
    pack_row(small[5][0], r, 0, row_sum(acc_e))
    pack_row(small[5][0], r, span, row_sum(acc_ex))
    red_a = BlockReduce(place, counts, big[0])
    local_a = big[0][0]
    stride_a = round_up(c0, 16)
    step_rows = 256
    for i in range(0, c0, step_rows):
        n = min(step_rows, c0 - i)
        value = dot(tin[:, i : i + n], cot_all, 0, 0)
        for j in range(0, trans, LANES):
            w = min(LANES, trans - j)
            local_a[j // LANES * stride_a + i : j // LANES * stride_a + i + n, 0:w] = value[:, j : j + w]

    total = red2.finish()
    mean2 = unpack_row(total, 0, bot) * per
    inv2 = lax.rsqrt(unpack_row(total, 2, bot) * per - mean2 * mean2 + EPSILON)
    half_a2 = 0.5 * gain2 * inv2
    half_b2 = 0.5 * shift2 - mean2 * half_a2
    red6.start()
    red_a.start()

    on_edges(lambda side: edge_copy(a2v, halo_sems, side, True).wait_send())

    def middle_body(t, carry):
        imgs = pl.ds(t * TILE_IMGS, TILE_IMGS)
        at = pl.ds(pl.multiple_of(t * tp, tp), tp)
        h = bnv[imgs].reshape(tp, bot) * half_a2 + half_b2
        th = jnp.tanh(h)
        ht = h * th
        mask = mv[at, 0:1]
        a2v[imgs, 1:5] = ((h + ht) * mask).astype(BF16).reshape(TILE_IMGS, 4, 16, bot)
        s2v[at, :] = ((1.0 + th) * (1.0 + (h - ht)) * (0.5 * mask)).astype(BF16)
        return carry

    lax.fori_loop(0, tiles, middle_body, 0)

    on_edges(lambda side: edge_copy(a2v, halo_sems, side, False).wait_recv())
    for side, row, fits, have in ((0, 0, inside_above, have_above), (1, 5, inside_below, have_below)):

        def edge_body(t, carry, side=side, row=row, fits=fits, have=have):
            size = 16
            imgs = pl.ds(pl.multiple_of(t * size, size), size)
            h = a2v[imgs, row].astype(F32).reshape(size * 16, bot) * half_a2 + half_b2
            value = h + h * jnp.tanh(h)
            mask = [jnp.where(flags[t * size + q] > 0, fits, 1.0) * have for q in range(size)]
            value = jnp.where(jnp.concatenate(mask, axis=0) > 0.0, value, 0.0)
            a2v[imgs, row] = value.astype(BF16).reshape(size, 16, bot)
            return carry

        lax.fori_loop(0, images // 16, edge_body, 0)
    red_a.step_b()
    red6.middle()

    col = lax.broadcasted_iota(jnp.int32, (tp, 1), 0) % 16
    not_first, not_last = jnp.where(col > 0, 1.0, 0.0), jnp.where(col < 15, 1.0, 0.0)

    def growth_body(t, carry):
        acc, acc2, acc_e, acc_eg = carry
        imgs = pl.ds(t * TILE_IMGS, TILE_IMGS)
        at, ct = pl.ds(pl.multiple_of(t * tp, tp), tp), pl.ds(pl.multiple_of(t * tc, tc), tc)
        z = dot(a2v[imgs, 0:4].reshape(tp, bot), wfm[0], 1, 0)
        z = z + dot(a2v[imgs, 1:5].reshape(tp, bot), wfm[1], 1, 0)
        z = z + dot(a2v[imgs, 2:6].reshape(tp, bot), wfm[2], 1, 0)
        left = pltpu.roll(z[:, 0:LANES], 1, 0) * not_first
        right = pltpu.roll(z[:, 2 * LANES :], tp - 1, 0) * not_last
        g = left + z[:, LANES : 2 * LANES] + right
        gv[at, :] = g
        gm = g * mv[at, :]
        high, low = split(gm)
        pg = dot(pmat[...], high, 1, 0) + dot(pmat[...], low, 1, 0)
        gt[ct, :] = pg
        e = eg[ct, :]
        return acc + fold_rows(pg), acc2 + fold_rows(gm * g), acc_e + fold_rows(e * pmv[ct, :]), acc_eg + fold_rows(e * pg)

    zero = jnp.zeros((8, LANES), F32)
    sums = lax.fori_loop(0, tiles, growth_body, (zero,) * 4)
    red3 = VectorReduce(place, counts, small[2])
    slot = small[2][0]
    for j in range(4):
        slot[r, j : j + 1, :] = row_sum(sums[j])
    red3.start()

    def part_body(t, carry):
        ct = pl.ds(pl.multiple_of(t * 256, 256), 256)
        px[ct, 0:trans] = dot(tin[ct, :], wlb[0:c0, :], 1, 0)
        return carry

    lax.fori_loop(0, n_cell // 256, part_body, 0)
    red3.middle()
    red_a.step_c()
    poolv[...] = jnp.zeros_like(poolv)
    for c in range(3):
        poolv[0:1, gr * c : gr * (c + 1)] = gaing
        poolv[1:2, gr * c : gr * (c + 1)] = shiftg
    gain_g, shift_g = poolv[0:1, :], poolv[1:2, :]
    total = red3.finish()
    mean_g = total[0:1, :] * per
    inv_g = lax.rsqrt(total[1:2, :] * per - mean_g * mean_g + EPSILON)
    shift_grad_g = total[2:3, :]
    gain_grad_g = inv_g * (0.25 * total[3:4, :] - mean_g * shift_grad_g)
    scale_g = gain_g * inv_g
    slope_g = scale_g * gain_grad_g * inv_g * per
    const_g = slope_g * mean_g - scale_g * shift_grad_g * per
    off_g = shift_g - mean_g * scale_g

    def grad_body(t, carry):
        imgs = pl.ds(t * TILE_IMGS, TILE_IMGS)
        at, ct = pl.ds(pl.multiple_of(t * tp, tp), tp), pl.ds(pl.multiple_of(t * tc, tc), tc)
        high, low = split(eg[ct, :] * (0.25 * scale_g) + const_g)
        wide = dot(umat[...], high, 1, 0) + dot(umat[...], low, 1, 0)
        gg = (wide - gv[at, :] * slope_g) * mv[at, :]
        ggv[imgs, 1:5] = gg.astype(BF16).reshape(TILE_IMGS, 4, 16, LANES)
        ting[ct, :] = (gt[ct, :] * (0.25 * scale_g) + pmv[ct, :] * off_g).astype(BF16)
        return carry

    lax.fori_loop(0, tiles, grad_body, 0)

    on_edges(lambda side: edge_copy(ggv, gg_sems, side, True).start())

    @pl.when(r == 0)
    def _():
        ggv[:, 0] = jnp.zeros((images, 16, LANES), BF16)

    @pl.when(r == rows - 1)
    def _():
        ggv[:, 5] = jnp.zeros((images, 16, LANES), BF16)

    lane = lax.broadcasted_iota(jnp.int32, (1, LANES), 1)

    def pool_body(t, carry):
        ct = pl.ds(pl.multiple_of(t * 256, 256), 256)
        own_g = jnp.where(lane < gr, ting[ct, :].astype(F32), 0.0).astype(BF16)
        value = px[ct, 0:trans] + dot(own_g, wlg[...], 1, 0)
        hpool[pl.ds(t * 16, 16)] = value.astype(BF16).reshape(16, 16, trans)
        return carry

    hpool = take(1)[0]
    lax.fori_loop(0, n_cell // 256, pool_body, 0)
    pool_copies = []
    for step in range(1, rows):
        peer = lax.rem(r + step, rows)
        pool_copies.append(
            pltpu.make_async_remote_copy(
                src_ref=hpool.at[pl.ds(peer * own, own)],
                dst_ref=cotv.at[pl.ds(r * own, own)],
                send_sem=pool_sems.at[0, step],
                recv_sem=pool_sems.at[1, step],
                device_id={"rows": peer},
                device_id_type=MESH,
            )
        )
    red_a.step_d()
    red_c = BlockReduce(place, counts, big[1])
    local_c[...] = jnp.zeros_like(local_c)
    base_c = len(tiles_c0) * round_up(bot, 8)
    stride_g = round_up(gr, 8)
    value = dot(ting[...], cot_all, 0, 0)
    for j in range(0, trans, LANES):
        w = min(LANES, trans - j)
        top = base_c + j // LANES * stride_g
        local_c[top : top + gr, 0:w] = value[0:gr, j : j + w]
    base_taps = base_c + -(-trans // LANES) * stride_g

    on_edges(lambda side: edge_copy(ggv, gg_sems, side, True).wait_send())
    on_edges(lambda side: edge_copy(ggv, gg_sems, side, False).wait_recv())
    lanes_all = lax.broadcasted_iota(jnp.int32, (tp, LANES), 1)
    wft[0] = jnp.zeros(wft.shape[1:], F32)

    def conv_body(t, carry):
        acc, acc2 = carry
        imgs = pl.ds(t * TILE_IMGS, TILE_IMGS)
        at = pl.ds(pl.multiple_of(t * tp, tp), tp)
        above = ggv[imgs, 0:4].reshape(tp, LANES).astype(F32)
        here = ggv[imgs, 1:5].reshape(tp, LANES).astype(F32)
        below = ggv[imgs, 2:6].reshape(tp, LANES).astype(F32)
        mixed = jnp.where(lanes_all < gr, below, jnp.where(lanes_all < 2 * gr, here, jnp.where(lanes_all < 3 * gr, above, 0.0)))
        from_right = pltpu.roll(mixed, tp - 1, 0) * not_last
        from_left = pltpu.roll(mixed, 1, 0) * not_first
        patch = jnp.concatenate([from_right, mixed, from_left], axis=1).astype(BF16)
        gm = dot(patch, wbm[...], 1, 0) * s2v[at, :].astype(F32)
        gmv[at, :] = gm
        wft[0] += dot(patch, a2v[imgs, 1:5].reshape(tp, bot), 0, 0)
        hat = bnv[imgs].reshape(tp, bot) - mean2
        return acc + fold_rows(gm), acc2 + fold_rows(gm * hat)

    zero = jnp.zeros((8, bot), F32)
    acc, acc2 = lax.fori_loop(0, tiles, conv_body, (zero, zero))
    red4 = VectorReduce(place, counts, small[3])
    slot = small[3][0]
    pack_row(slot, r, 0, row_sum(acc))
    pack_row(slot, r, 2, row_sum(acc2))
    red4.start()
    red4.middle()
    for copy in pool_copies:
        copy.start()
    pool_own = pltpu.make_async_copy(
        hpool.at[pl.ds(r * own, own)], pool_hbm.at[:, pl.ds(pl.multiple_of(r * 16, 16), 16)], io_sems.at[4]
    )
    pool_own.start()
    red_a.step_e()
    gap = lax.broadcasted_iota(jnp.int32, (bot, 9 * bot), 1) - 9 * lax.broadcasted_iota(jnp.int32, (bot, 9 * bot), 0)
    value = jnp.zeros((gr, 9 * bot), F32)
    for dh in range(3):
        for dw in range(3):
            pick = jnp.where(gap == 3 * dh + dw, 1.0, 0.0).astype(BF16)
            tap = wft[0, LANES * dw + gr * dh : LANES * dw + gr * (dh + 1), :]
            high, low = split(tap)
            value = value + (dot(high, pick, 1, 0) + dot(low, pick, 1, 0))
    for j in range(0, 9 * bot, LANES):
        w = min(LANES, 9 * bot - j)
        top = base_taps + j // LANES * stride_g
        local_c[top : top + gr, 0:w] = value[:, j : j + w]
    total = red4.finish()
    shift_grad2 = unpack_row(total, 0, bot)
    gain_grad2 = inv2 * unpack_row(total, 2, bot)
    scale2 = gain2 * inv2
    slope2 = scale2 * gain_grad2 * inv2 * per
    const2 = scale2 * shift_grad2 * per - slope2 * mean2

    stride_f = round_up(bot, 8)
    blocks = -(-c0 // LANES)

    def bottleneck_body(t, carry):
        imgs = pl.ds(t * TILE_IMGS, TILE_IMGS)
        at = pl.ds(pl.multiple_of(t * tp, tp), tp)
        bn = bnv[imgs].reshape(tp, bot)
        gb = ((gmv[at, :] * scale2 - bn * slope2 - const2) * mv[at, 0:1]).astype(BF16)
        s2v[at, :] = gb
        grad = dot(gb, av[at, :], 0, 0)
        for k, (j, w) in enumerate(tiles_c0):
            local_b[k * stride_f : k * stride_f + bot, 0:w] += grad[:, j : j + w]
        return carry

    lax.fori_loop(0, tiles, bottleneck_body, 0)
    red_c.start()

    def back_body(t, carry):
        acc, acc2 = carry
        at = pl.ds(pl.multiple_of(t * tp, tp), tp)
        gb = s2v[at, :]
        sums, cross = [], []
        for k, (j, w) in enumerate(blocks_c0):
            cols = slice(j, j + w)
            value = dot(gb, wfb[:, cols], 1, 0)
            total, total2 = acc[k], acc2[k]
            for i in range(0, tp, 32):
                part = pl.ds(pl.multiple_of(t * tp + i, 32), 32)
                gf = value[i : i + 32] * sv[part, cols].astype(F32)
                av[part, cols] = gf.astype(BF16)
                total = total + fold_rows(gf)
                total2 = total2 + fold_rows(gf * xv[part, cols].astype(F32))
            sums.append(total)
            cross.append(total2)
        return tuple(sums), tuple(cross)

    zero = zeros_for(blocks_c0)
    sums = lax.fori_loop(0, tiles // 2, back_body, (zero, zero))
    red_c.step_b()
    sums = lax.fori_loop(tiles // 2, tiles, back_body, sums)
    acc, acc2 = jnp.concatenate(sums[0], axis=1), jnp.concatenate(sums[1], axis=1)
    red5 = VectorReduce(place, counts, small[4])
    pack_row(small[4][0], r, 0, row_sum(acc))
    pack_row(small[4][0], r, span, row_sum(acc2))
    red5.start()
    red_c.step_c()
    cvec[0:1, 0:c0] = 0.25 * cvec[7:8, 0:c0]
    cvec[2:3, 0:c0] = 0.5 * cvec[6:7, 0:c0]

    def part_grad(t, carry):
        for q in range(TILE_IMGS):
            img = t * TILE_IMGS + q
            for j, w in tiles_c0:
                cols, full = slice(j, j + w), slice(j, j + LANES)
                ct = pl.ds(pl.multiple_of(img * 16, 16), 16)
                cells = ev[ct, full] * cvec[0:1, full] * pmv[ct, :]
                up[j // LANES, pl.ds(0, 16, stride=2), :] = cells
                up[j // LANES, pl.ds(1, 16, stride=2), :] = cells
                scale = cvec[2:3, cols]
                for half in range(2):
                    at = pl.ds(pl.multiple_of(img * 64 + half * 32, 32), 32)
                    wide_cells = up[j // LANES, half * 16 : half * 16 + 16, 0:w]
                    wide_cells = jnp.concatenate([wide_cells, wide_cells], axis=0)
                    sv[at, cols] = (wide_cells + av[at, cols].astype(F32) * scale).astype(BF16)
        return carry

    lax.fori_loop(0, tiles // 4, part_grad, 0)
    red5.middle()
    lax.fori_loop(tiles // 4, 7 * tiles // 12, part_grad, 0)
    red_c.step_d()
    lax.fori_loop(7 * tiles // 12, tiles, part_grad, 0)
    red_a.step_f()
    total = red5.finish()
    red_c.step_e()
    pool_outs = [pool_own]
    for step in range(1, rows):
        pool_copies[step - 1].wait()
        sender = lax.rem(r + rows - step, rows)
        dst = pool_hbm.at[:, pl.ds(pl.multiple_of(sender * 16, 16), 16)]
        pool_outs.append(pltpu.make_async_copy(cotv.at[pl.ds(sender * own, own)], dst, pool_sems.at[2, step]))
        pool_outs[-1].start()
    mean1, inv1 = cvec[4:5, 0:c0], cvec[5:6, 0:c0]
    scale1, scale3 = cvec[6:7, 0:c0], cvec[7:8, 0:c0]
    shift_grad1 = 0.5 * unpack_row(total, 0, c0)
    gain_grad1 = inv1 * (0.5 * unpack_row(total, span, c0) - mean1 * shift_grad1)
    total = red6.finish()
    shift_grad3 = unpack_row(total, 0, c0)
    gain_grad3 = inv1 * (0.25 * unpack_row(total, span, c0) - mean1 * shift_grad3)
    slope1 = (scale3 * gain_grad3 + scale1 * gain_grad1) * inv1 * per
    const1 = (scale3 * shift_grad3 + scale1 * shift_grad1) * per - slope1 * mean1
    stats[...] = jnp.zeros_like(stats)
    stats[0:1, 0:c0] = gain_grad1
    stats[1:2, 0:c0] = shift_grad1
    stats[2:3, 0:bot] = gain_grad2
    stats[3:4, 0:bot] = shift_grad2
    stats[4:5, 0:c0] = gain_grad3
    stats[5:6, 0:c0] = shift_grad3
    stats[6:7, 0:LANES] = gain_grad_g
    stats[7:8, 0:LANES] = shift_grad_g
    stats[8:9, :] = jnp.broadcast_to(count_all, (1, stats.shape[1]))
    cvec[1:2, 0:c0] = const1
    cvec[3:4, 0:c0] = slope1

    def out_copy(t):
        at = pl.ds(pl.multiple_of(t * tp, tp), tp)
        return pltpu.make_async_copy(av.at[at], ig_hbm.at[at], x_sems.at[t])

    def last_body(t, carry):
        for q in range(TILE_IMGS):
            img = t * TILE_IMGS + q
            for j, w in tiles_c0:
                cols = slice(j, j + w)
                slope, const = cvec[3:4, cols], cvec[1:2, cols]
                for i in range(0, 64, 32):
                    at = pl.ds(pl.multiple_of(img * 64 + i, 32), 32)
                    value = (xv[at, cols].astype(F32) * slope + const) * mv[at, 0:w]
                    av[at, cols] = (sv[at, cols].astype(F32) - value).astype(BF16)
        out_copy(t).start()
        return carry

    lax.fori_loop(0, tiles // 2, last_body, 0)
    red_c.step_f()
    lax.fori_loop(tiles // 2, tiles, last_body, 0)
    red_a.finish()
    out_a = pltpu.make_async_copy(big[0][5], sum_a, io_sems.at[0])
    out_a.start()
    red_c.finish()
    out_c = pltpu.make_async_copy(big[1][5], sum_c, io_sems.at[2])
    out_c.start()
    for copy in pool_outs:
        copy.wait()
    for t in range(tiles):
        out_copy(t).wait()
    out_a.wait()
    out_c.wait()


def mm3(a, b, ca, cb):
    left = jnp.concatenate([a[0], a[0], a[1]], axis=ca)
    right = jnp.concatenate([b[0], b[1], b[0]], axis=cb)
    return dot(left, right, ca, cb)


def orthogonal_steps(pads, sides, sizes, found):
    start, gram, prod, ones = [], [], [], []
    for pad, side, size in zip(pads, sides, sizes):
        halves = unit_norm(pad)
        start.append(halves)
        gram.append(mm3(halves, halves, side, side))
        full = gram[-1].shape[0]
        i, j = (lax.broadcasted_iota(jnp.int32, (full, full), d) for d in (0, 1))
        ones.append((i == j) & (i < size))
        prod.append(None)
    yield
    for k in range(NS_STEPS):
        halves = [split(g) for g in gram]
        square = [mm3(h, h, 1, 0) for h in halves]
        poly = [jnp.where(o, QUINTIC_A, 0.0) + QUINTIC_B * g + QUINTIC_C * s for o, g, s in zip(ones, gram, square)]
        poly_h = [split(p) for p in poly]
        if k < NS_STEPS - 1:
            mid = [split(mm3(h, p, 1, 0)) for h, p in zip(halves, poly_h)]
            gram = [mm3(m, p, 1, 0) for m, p in zip(mid, poly_h)]
        prod = [p if k == 0 else split(mm3(q, p, 1, 0)) for q, p in zip(prod, poly_h)]
        if k == NS_STEPS - 1:
            found.extend(zip(start, prod))
        yield


def unit_norm(pad):
    value = pad[...]
    norm = jnp.sqrt(jnp.sum(jnp.sum(value * value, axis=0, keepdims=True), axis=1, keepdims=True)) + TINY
    pad[...] = value / norm
    return split(pad[...])


class LoopedOrthogonal:
    def __init__(self, valid, refs):
        self.valid = valid
        self.stack, self.poly, self.mid = refs
        self.full = self.poly.shape[1]

    @staticmethod
    def scratch(full):
        return [pltpu.VMEM((2, 2 * full, full), BF16), pltpu.VMEM((2, full, full), BF16), pltpu.VMEM((2, full, full), BF16)]

    def store(self, ref, start, value):
        high, low = split(value)
        ref[0, start : start + value.shape[0]] = high
        ref[1, start : start + value.shape[0]] = low

    def unit(self, scale):
        i, j = (lax.broadcasted_iota(jnp.int32, (self.full, self.full), d) for d in (0, 1))
        return jnp.where((i == j) & self.valid(i), scale, 0.0)

    def begin(self, gram):
        self.store(self.stack, 0, gram)
        self.stack[0, self.full :] = self.unit(1.0).astype(BF16)
        self.stack[1, self.full :] = jnp.zeros((self.full, self.full), BF16)

    def polynomial(self):
        n = self.full
        high, low = self.stack[0, 0:n], self.stack[1, 0:n]
        square = mm3((high, low), (high, low), 1, 0)
        gram = high.astype(F32) + low.astype(F32)
        self.store(self.poly, 0, self.unit(QUINTIC_A) + QUINTIC_B * gram + QUINTIC_C * square)

    def step(self, k, carry):
        n = self.full
        self.polynomial()
        poly = (self.poly[0], self.poly[1])
        both = mm3((self.stack[0], self.stack[1]), poly, 1, 0)
        self.store(self.mid, 0, both[0:n])
        self.store(self.stack, n, both[n:])
        self.store(self.stack, 0, mm3((self.mid[0], self.mid[1]), poly, 1, 0))
        return carry

    def light_step(self, k, carry):
        n = self.full
        high = self.stack[0, 0:n]
        gram = high.astype(F32) + self.stack[1, 0:n].astype(F32)
        poly = (QUINTIC_B * gram + QUINTIC_C * dot(high, high, 1, 0)).astype(BF16)
        self.poly[0] = poly
        both = self.stack[0].astype(F32) + self.stack[1].astype(F32)
        both = QUINTIC_A * both + dot(self.stack[0], poly, 1, 0)
        self.store(self.stack, n, both[n:])
        mid = both[0:n]
        self.store(self.stack, 0, QUINTIC_A * mid + dot(mid.astype(BF16), self.poly[0], 1, 0))
        return carry

    def finish(self):
        n = self.full
        self.polynomial()
        return split(mm3((self.stack[0, n:], self.stack[1, n:]), (self.poly[0], self.poly[1]), 1, 0))


def sum_rows(ref, top, count, width):
    base = top // 16 * 16
    size = min(round_up(top - base + count, 16), ref.shape[0] - base)
    return ref[base : base + size, :].astype(F32)[top - base : top - base + count, 0:width]


def transition_moment(c0, gr, trans, ml, sum_a, sum_c, base, put):
    stride_a, stride_g = round_up(c0, 16), round_up(gr, 8)
    for j, w in lane_tiles(trans):
        k = j // LANES
        put(slice(0, c0), slice(j, j + w), MOMENTUM_DECAY * ml[0:c0, j : j + w] + sum_rows(sum_a, k * stride_a, c0, w))
        rows = slice(c0, c0 + gr)
        put(rows, slice(j, j + w), MOMENTUM_DECAY * ml[rows, j : j + w] + sum_rows(sum_c, base + k * stride_g, gr, w))


def update_kernel(dims, ig_in, pool_in, wl_hbm, ml_hbm, stats, sum_a, sum_c, params, p_moment, wf, wg, mf, mg, *refs):
    (c0, bot, gr, trans) = dims
    cat = c0 + gr
    (ig_out, pool_out, wl_out, ml_out, p_moment_new, params_new, mf_new, mg_new, wf_new, wg_new) = refs[:10]
    (lpad, spad, igv, poolv, wl, ml, sems) = refs[10:17]
    low = round_up(bot, 8)
    loops = [
        LoopedOrthogonal(lambda i: i < trans, refs[17:20]),
        LoopedOrthogonal(lambda i: (i < bot) | ((i >= low) & (i < low + gr)), refs[20:23]),
    ]
    loads = [pltpu.make_async_copy(ml_hbm, ml, sems.at[0, 0]), pltpu.make_async_copy(wl_hbm, wl, sems.at[0, 1])]
    loads += [pltpu.make_async_copy(ig_in, igv, sems.at[0, 2]), pltpu.make_async_copy(pool_in, poolv, sems.at[0, 3])]
    stores = [pltpu.make_async_copy(ml, ml_out, sems.at[1, 0]), pltpu.make_async_copy(wl, wl_out, sems.at[1, 1])]
    stores += [pltpu.make_async_copy(igv, ig_out, sems.at[1, 2]), pltpu.make_async_copy(poolv, pool_out, sems.at[1, 3])]
    for copy in loads:
        copy.start()

    count = stats[8:9, 0:1]
    step = NORM_RATE * lax.rsqrt(count)
    spans = ((0, c0, 0), (c0, bot, 2), (c0 + bot, c0, 4), (2 * c0 + bot, gr, 6))
    for start, width, row in spans:
        moment = MOMENTUM_DECAY * p_moment[:, start : start + width] + stats[row : row + 2, 0:width]
        p_moment_new[:, start : start + width] = moment
        params_new[:, start : start + width] = params[:, start : start + width] - step * moment

    stride_g, stride_f = round_up(gr, 8), round_up(bot, 8)
    lpad[...] = jnp.zeros_like(lpad)
    spad[...] = jnp.zeros_like(spad)
    base = len(lane_tiles(c0)) * stride_f
    for j, w in lane_tiles(c0):
        new = MOMENTUM_DECAY * mf[:, j : j + w] + sum_rows(sum_c, j // LANES * stride_f, bot, w)
        mf_new[:, j : j + w] = new
        spad[0:bot, j : j + w] = new
    loads[0].wait()

    def put(at, cols, value):
        ml[at, cols] = value
        lpad[at, cols] = value

    transition_moment(c0, gr, trans, ml, sum_a, sum_c, base, put)
    stores[0].start()
    base = base + len(lane_tiles(trans)) * stride_g
    for j, w in lane_tiles(9 * bot):
        new = MOMENTUM_DECAY * mg[:, j : j + w] + sum_rows(sum_c, base + j // LANES * stride_g, gr, w)
        mg_new[:, j : j + w] = new
        spad[low : low + gr, j : j + w] = new
    halves = unit_norm(lpad)
    loops[0].begin(mm3(halves, halves, 0, 0))
    norms = []
    for start, stop in ((0, low), (low, low + round_up(gr, 8))):
        value = spad[start:stop, :]
        total = jnp.sum(jnp.sum(value * value, axis=0, keepdims=True), axis=1, keepdims=True)
        norms.append(1.0 / (jnp.sqrt(total) + TINY))
    row = lax.broadcasted_iota(jnp.int32, (spad.shape[0], 1), 0)
    spad[...] = spad[...] * jnp.where(row < low, norms[0], norms[1])
    halves = split(spad[...])
    gram = mm3(halves, halves, 1, 1)
    i, j = (lax.broadcasted_iota(jnp.int32, gram.shape, d) for d in (0, 1))
    loops[1].begin(jnp.where((i < low) == (j < low), gram, 0.0))
    for k in (2, 3):
        loads[k].wait()
        stores[k].start()

    def light(k, carry):
        loops[0].light_step(k, carry)
        loops[1].step(k, carry)
        return carry

    def full(k, carry):
        for loop in loops:
            loop.step(k, carry)
        return carry

    lax.fori_loop(0, 2, light, 0)
    lax.fori_loop(2, 4, full, 0)
    prods = [loop.finish() for loop in loops]
    ortho = mm3(split(lpad[...]), prods[0], 1, 0)
    loads[1].wait()
    wl[...] = wl[...] - MUON_RATE * ortho[0:cat, 0:trans]
    stores[1].start()
    ortho = mm3(prods[1], split(spad[...]), 1, 0)
    wf_new[...] = wf[...] - MUON_RATE * ortho[0:bot, 0:c0]
    wg_new[...] = wg[...] - MUON_RATE * ortho[low : low + gr, 0 : 9 * bot]
    for copy in stores:
        copy.wait()


def per_device(counts, inputs, small_flags, norm_params, norm_moment, w_bottleneck, w_growth, w_transition,
               m_bottleneck, m_growth, m_transition, cotangent):
    rows, batch = counts
    images, band, width, c0 = inputs.shape
    bot, gr, trans = w_bottleneck.shape[1], w_growth.shape[1], w_transition.shape[1]
    own = cotangent.shape[0]
    cat = c0 + gr
    n_pix, n_cell = images * 64, images * 16
    assert rows == 4 and band == 4 and width == 16 and images % 16 == 0
    any_spec = pl.BlockSpec(memory_space=pl.ANY)
    vmem_spec = pl.BlockSpec(memory_space=pltpu.VMEM)
    smem_spec = pl.BlockSpec(memory_space=pltpu.SMEM)
    wide = round_up(c0, LANES)
    unit = 16 * 4 * batch
    blocks = -(-trans // LANES)
    rows_b = -(-c0 // LANES) * round_up(bot, 8)
    rows_c = (blocks + -(-9 * bot // LANES)) * round_up(gr, 8)
    length_a = round_up(blocks * round_up(c0, 16), unit)
    length_c = round_up(rows_b + rows_c, unit)
    dims = (rows, batch, images, c0, bot, gr, trans, own)
    v = pltpu.VMEM
    dma = pltpu.SemaphoreType.DMA

    def vector_scratch(height):
        return [v((rows, height, LANES), F32), v((batch, height, LANES), F32), dma((2, rows)), dma((2, batch))]

    scratch = [
        v((n_pix, c0), BF16), v((n_pix, c0), BF16), v((n_pix, c0), BF16),
        v((n_pix, LANES), F32), v((n_cell, LANES), F32),
        v((n_cell, c0), F32), v((n_cell, c0), BF16), v((n_cell, LANES), BF16),
        v((n_cell, wide), F32), v((n_cell, LANES), F32), v((images, 16, trans), BF16),
        v((images, 4, 16, bot), F32),
        v((images, 6, 16, bot), BF16), v((n_pix, bot), BF16), v((n_pix, LANES), F32),
        v((images, 6, 16, LANES), BF16), v((n_pix, bot), F32),
        v((cat, trans), F32), v((cat, trans), BF16), v((LANES, trans), BF16),
        v((bot, c0), F32), v((bot, c0), BF16), v((c0, bot), BF16), v((gr, 9 * bot), F32),
        v((4, 3 * LANES, bot), F32), v((3, bot, 3 * LANES), BF16), v((3 * LANES, bot), BF16),
        v((TILE_IMGS * 16, TILE_IMGS * 64), BF16), v((TILE_IMGS * 64, TILE_IMGS * 16), BF16),
        v((8, wide), F32), v((8, LANES), F32), v((n_cell, LANES), F32),
        dma((images // TILE_IMGS,)), dma((5,)), dma((2, rows)), dma((2, 2)), dma((2, 2)), dma((3, rows)),
    ]
    for height in (16, 8, 8, 8):
        scratch += vector_scratch(height)
    scratch += [dma((2, rows)), dma((2, batch))] + vector_scratch(16)
    for length in (length_a, length_c):
        scratch += BlockReduce.scratch(length, batch)
    scratch += [v((wide // LANES, 32, LANES), F32)]
    scratch += [v((images, 16, trans), BF16)]
    struct = jax.ShapeDtypeStruct
    input_grad, pooled, stats, sum_a, sum_c = pl.pallas_call(
        functools.partial(band_kernel, dims),
        out_shape=(
            struct((n_pix, c0), BF16),
            struct((own, 64, trans), BF16),
            struct((16, wide), F32),
            struct((length_a, LANES), BF16),
            struct((length_c, LANES), BF16),
        ),
        in_specs=[smem_spec, any_spec, any_spec, vmem_spec, any_spec, any_spec, any_spec],
        out_specs=[any_spec, any_spec, vmem_spec, any_spec, any_spec],
        scratch_shapes=scratch,
        compiler_params=pltpu.CompilerParams(collective_id=0, has_side_effects=True, vmem_limit_bytes=VMEM_BYTES),
        name="band",
    )(
        small_flags,
        inputs.reshape(n_pix, c0),
        cotangent.reshape(own, 64, trans),
        norm_params,
        w_bottleneck.T,
        w_growth.T,
        w_transition,
    )
    vectors = [struct(norm_params.shape, F32)] * 2
    weights = [struct((bot, c0), F32), struct((gr, 9 * bot), F32)]
    outs = pl.pallas_call(
        functools.partial(update_kernel, (c0, bot, gr, trans)),
        out_shape=[struct((n_pix, c0), BF16), struct((own, 64, trans), BF16)]
        + [struct((cat, trans), F32)] * 2
        + vectors
        + weights * 2,
        in_specs=[any_spec] * 4 + [vmem_spec] * 9,
        out_specs=[any_spec] * 4 + [vmem_spec] * 6,
        scratch_shapes=[
            v((round_up(cat, 128), 4 * LANES), F32),
            v((round_up(bot + gr + 16, 256), round_up(max(c0, 9 * bot), LANES)), F32),
            v((n_pix, c0), BF16),
            v((own, 64, trans), BF16),
            v((cat, trans), F32),
            v((cat, trans), F32),
            dma((2, 4)),
        ]
        + LoopedOrthogonal.scratch(4 * LANES)
        + LoopedOrthogonal.scratch(round_up(bot + gr + 16, 256)),
        compiler_params=pltpu.CompilerParams(vmem_limit_bytes=VMEM_BYTES),
        name="update",
    )(
        input_grad, pooled, w_transition, m_transition, stats, sum_a, sum_c, norm_params, norm_moment, w_bottleneck.T,
        w_growth.T, m_bottleneck.T, m_growth.T,
    )
    (ig, pooled, wl_new, ml_new, moment_new, params_new, mf_new, mg_new, wf_new, wg_new) = outs
    return (
        pooled.reshape(cotangent.shape),
        ig.reshape(inputs.shape),
        moment_new,
        params_new,
        mf_new.T,
        mg_new.T,
        ml_new,
        wf_new.T,
        wg_new.T,
        wl_new,
    )


def solution(mesh):
    counts = (mesh.shape["rows"], mesh.shape["batch"])
    whole = (P(),) * 8
    images = P(("batch", "rows"), None, None, None)
    bands = P("batch", "rows", None, None)
    return jax.shard_map(
        functools.partial(per_device, counts),
        mesh=mesh,
        in_specs=(bands, P("batch")) + whole + (images,),
        out_specs=(images, bands) + whole,
        check_vma=False,
    )
```

```python
import functools

import jax
import jax.numpy as jnp
from jax import lax
from jax.experimental import pallas as pl
from jax.experimental.pallas import tpu as pltpu
from jax.sharding import PartitionSpec as P

SMALL = 12
NS_STEPS = 5
EPSILON = 1e-05
MOMENTUM_DECAY = 0.9
MUON_RATE = 0.5
NORM_RATE = 1.0
QUINTIC_A = 3.4445
QUINTIC_B = -4.775
QUINTIC_C = 2.0315
TINY = 1e-07
F32 = jnp.float32
BF16 = jnp.bfloat16
MESH = pl.DeviceIdType.MESH
LANES = 128
TILE_IMGS = 8
VMEM_BYTES = 62 * 1024 * 1024


def dot(a, b, ca, cb):
    return lax.dot_general(a, b, (((ca,), (cb,)), ((), ())), preferred_element_type=F32)


def split(a):
    high = a.astype(BF16)
    return high, (a - high.astype(F32)).astype(BF16)


def round_up(value, step):
    return -(-value // step) * step


def fold_rows(value):
    rows, cols = value.shape
    return jnp.sum(value.reshape(rows // 8, 8, cols), axis=0)


def lane_tiles(total):
    return [(j, min(LANES, total - j)) for j in range(0, total, LANES)]


def lane_blocks(total):
    return [(j, min(2 * LANES, total - j)) for j in range(0, total, 2 * LANES)]


def zeros_for(pieces):
    return tuple(jnp.zeros((8, w), F32) for _, w in pieces)


def pack_row(slots, r, top, row):
    for k, (j, w) in enumerate(lane_tiles(row.shape[1])):
        slots[r, top + k : top + k + 1, 0:w] = row[:, j : j + w]


def unpack_row(total, top, size):
    return jnp.concatenate([total[top + k : top + k + 1, 0:w] for k, (_, w) in enumerate(lane_tiles(size))], axis=1)


def row_sum(value):
    return jnp.sum(value, axis=0, keepdims=True)


class VectorReduce:
    def __init__(self, place, counts, refs):
        self.r, self.b = place
        self.rows, self.batch = counts
        self.row_slots, self.batch_slots, self.row_sems, self.batch_sems = refs

    def copies(self, axis, me, count, slots, sems):
        made = []
        for step in range(1, count):
            peer = lax.rem(me + step, count)
            made.append(
                pltpu.make_async_remote_copy(
                    src_ref=slots.at[me],
                    dst_ref=slots.at[me],
                    send_sem=sems.at[0, step],
                    recv_sem=sems.at[1, step],
                    device_id={axis: peer},
                    device_id_type=MESH,
                )
            )
        return made

    def start(self):
        self.first = self.copies("rows", self.r, self.rows, self.row_slots, self.row_sems)
        for copy in self.first:
            copy.start()

    def middle(self):
        for copy in self.first:
            copy.wait_recv()
        total = self.row_slots[0]
        for j in range(1, self.rows):
            total = total + self.row_slots[j]
        self.batch_slots[self.b] = total
        self.second = self.copies("batch", self.b, self.batch, self.batch_slots, self.batch_sems)
        for copy in self.second:
            copy.start()

    def finish(self):
        for copy in self.second:
            copy.wait_recv()
        total = self.batch_slots[0]
        for j in range(1, self.batch):
            total = total + self.batch_slots[j]
        for copy in self.first + self.second:
            copy.wait_send()
        return total


class BlockReduce:
    def __init__(self, place, counts, refs):
        self.r, self.b = place
        self.batch = counts[1]
        self.local, self.out_a, self.in_a, self.in_b, self.in_c, self.full, self.sems = refs
        self.length = self.local.shape[0]
        self.out_b = self.out_a.at[pl.ds(0, self.length // 4)]
        self.out_c = self.out_a.at[pl.ds(self.length // 4, self.length // 4)]
        self.chunk = self.length // (4 * self.batch)
        self.low, self.high = lax.rem(self.r, 2), lax.div(self.r, 2)
        self.near = self.r + 1 - 2 * self.low
        self.far = self.r + 2 - 4 * self.high

    def each(self, count, body):
        step = 16
        for size in (256, 128, 64, 32):
            if count % size == 0:
                step = size
                break

        def run(i, carry):
            body(pl.multiple_of(i * step, 16), step)
            return carry

        lax.fori_loop(0, count // step, run, 0)

    def copy(self, src, dst, axis, peer, slot):
        return pltpu.make_async_remote_copy(
            src_ref=src,
            dst_ref=dst,
            send_sem=self.sems.at[0, slot],
            recv_sem=self.sems.at[1, slot],
            device_id={axis: peer},
            device_id_type=MESH,
        )

    def at(self, start, size):
        return pl.ds(pl.multiple_of(start, 16), size)

    def start(self):
        half = self.length // 2
        other = (1 - self.low) * half

        def body(i, n):
            self.out_a[self.at(i, n)] = self.local[self.at(other + i, n)].astype(BF16)

        self.each(half, body)
        self.a = self.copy(self.out_a, self.in_a, "rows", self.near, 0)
        self.a.start()

    def step_b(self):
        quarter = self.length // 4
        self.a.wait()
        other = (1 - self.high) * quarter
        mine = self.low * 2 * quarter

        def body(i, n):
            total = self.local[self.at(mine + other + i, n)] + self.in_a[self.at(other + i, n)].astype(F32)
            self.out_b[self.at(i, n)] = total.astype(BF16)

        self.each(quarter, body)
        self.b_copy = self.copy(self.out_b, self.in_b, "rows", self.far, 1)
        self.b_copy.start()

    def step_c(self):
        quarter = self.length // 4
        self.b_copy.wait()
        mine = self.low * 2 * quarter + self.high * quarter

        def body(i, n):
            total = self.local[self.at(mine + i, n)] + self.in_a[self.at(self.high * quarter + i, n)].astype(F32)
            total = total + self.in_b[self.at(i, n)].astype(F32)
            self.local[self.at(mine + i, n)] = total
            self.out_c[self.at(i, n)] = total.astype(BF16)

        self.each(quarter, body)
        self.c = []
        for step in range(1, self.batch):
            peer = lax.rem(self.b + step, self.batch)
            piece = self.out_c.at[self.at(peer * self.chunk, self.chunk)]
            self.c.append(self.copy(piece, self.in_c.at[step], "batch", peer, 1 + step))
        for copy in self.c:
            copy.start()

    def step_d(self):
        quarter = self.length // 4
        for copy in self.c:
            copy.wait()
        mine = self.low * 2 * quarter + self.high * quarter + self.b * self.chunk

        def body(i, n):
            total = self.local[self.at(mine + i, n)]
            for step in range(1, self.batch):
                total = total + self.in_c[step, self.at(i, n)].astype(F32)
            self.full[self.at(mine + i, n)] = total.astype(BF16)

        self.each(self.chunk, body)
        piece = self.full.at[self.at(mine, self.chunk)]
        self.d = []
        for step in range(1, self.batch):
            peer = lax.rem(self.b + step, self.batch)
            self.d.append(self.copy(piece, piece, "batch", peer, self.batch + step))
        for copy in self.d:
            copy.start()

    def step_e(self):
        quarter = self.length // 4
        for copy in self.d:
            copy.wait()
        self.e_copy().start()

    def e_copy(self):
        quarter = self.length // 4
        piece = self.full.at[self.at(self.low * 2 * quarter + self.high * quarter, quarter)]
        return self.copy(piece, piece, "rows", self.far, 2 * self.batch)

    def step_f(self):
        half = self.length // 2
        self.e_copy().wait()
        piece = self.full.at[self.at(self.low * half, half)]
        self.f = self.copy(piece, piece, "rows", self.near, 2 * self.batch + 1)
        self.f.start()

    def finish(self):
        self.f.wait()

    @staticmethod
    def scratch(length, batch):
        shapes = (length // 2, length // 2, length // 4)
        return (
            [pltpu.VMEM((length, LANES), F32)]
            + [pltpu.VMEM((n, LANES), BF16) for n in shapes]
            + [
                pltpu.VMEM((batch, length // (4 * batch), LANES), BF16),
                pltpu.VMEM((length, LANES), BF16),
                pltpu.SemaphoreType.DMA((2, 2 * batch + 2)),
            ]
        )


def band_kernel(dims, flags, x_hbm, cot_hbm, params, wf_hbm, wg_hbm, wl_hbm, *rest):
    (rows, batch, images, c0, bot, gr, trans, own) = dims
    cat = c0 + gr
    (ig_hbm, pool_hbm, stats, sum_a, sum_c) = rest[:5]
    rest = list(rest[5:])

    def take(n):
        taken = rest[:n]
        del rest[:n]
        return taken

    (xv, av, sv, mv, pmv, px, tin, ting, ev, eg, cotv) = take(11)
    (bnv, a2v, s2v, gv, ggv, gmv) = take(6)
    (wlf, wlb, wlg, wff, wfb, wfn, wgf, wft, wfm, wbm, pmat, umat, cvec, poolv, gt) = take(15)
    (x_sems, io_sems, cot_sems, halo_sems, gg_sems, pool_sems) = take(6)
    small = [take(4) for _ in range(4)]
    small.append(small[0][:2] + take(2))
    small.append(take(4))
    big = [take(7) for _ in range(2)]
    up = take(1)[0]
    local_b = local_c = big[1][0]

    r, b = lax.axis_index("rows"), lax.axis_index("batch")
    place, counts = (r, b), (rows, batch)
    n_pix, n_cell = images * 64, images * 16
    tiles = images // TILE_IMGS
    tp, tc = TILE_IMGS * 64, TILE_IMGS * 16

    w_copies = [
        pltpu.make_async_copy(wf_hbm, wff, io_sems.at[0]),
        pltpu.make_async_copy(wg_hbm, wgf, io_sems.at[1]),
        pltpu.make_async_copy(wl_hbm, wlf, io_sems.at[2]),
    ]
    w_copies[1].start()
    x_copies = [
        pltpu.make_async_copy(x_hbm.at[pl.ds(pl.multiple_of(t * tp, tp), tp)], xv.at[pl.ds(pl.multiple_of(t * tp, tp), tp)], x_sems.at[t]) for t in range(tiles)
    ]
    for copy in x_copies:
        copy.start()
    w_copies[0].start()
    w_copies[2].start()
    cot_own = pltpu.make_async_copy(
        cot_hbm.at[:, pl.ds(pl.multiple_of(r * 16, 16), 16)], cotv.at[pl.ds(r * own, own)], io_sems.at[3]
    )
    cot_own.start()
    barrier = pltpu.get_barrier_semaphore()
    for axis, me, count in (("rows", r, rows), ("batch", b, batch)):
        for step in range(1, count):
            pl.semaphore_signal(barrier, inc=1, device_id={axis: lax.rem(me + step, count)}, device_id_type=MESH)

    a_id = lax.broadcasted_iota(jnp.int32, (tc, tp), 0)
    b_id = lax.broadcasted_iota(jnp.int32, (tc, tp), 1)
    hit = (a_id // 8 == b_id // 32) & (a_id % 8 == (b_id % 16) // 2)
    pmat[...] = jnp.where(hit, 1.0, 0.0).astype(BF16)
    a_id = lax.broadcasted_iota(jnp.int32, (tp, tc), 1)
    b_id = lax.broadcasted_iota(jnp.int32, (tp, tc), 0)
    hit = (a_id // 8 == b_id // 32) & (a_id % 8 == (b_id % 16) // 2)
    umat[...] = jnp.where(hit, 1.0, 0.0).astype(BF16)

    pix = lax.broadcasted_iota(jnp.int32, (64, 1), 0)
    inside = jnp.where((r * 4 + pix // 16 < SMALL) & (pix % 16 < SMALL), 1.0, 0.0)
    cell = lax.broadcasted_iota(jnp.int32, (16, 1), 0)
    inside_cell = jnp.where((r * 4 + cell // 8 * 2 < SMALL) & (cell % 8 * 2 < SMALL), 1.0, 0.0)
    inside_above = jnp.where((r * 4 - 1 < SMALL) & (cell < SMALL), 1.0, 0.0)
    inside_below = jnp.where((r * 4 + 4 < SMALL) & (cell < SMALL), 1.0, 0.0)
    have_above = jnp.where(r > 0, 1.0, 0.0)
    have_below = jnp.where(r < rows - 1, 1.0, 0.0)
    inside_count = jnp.clip(SMALL - r * 4, 0, 4) * SMALL

    copy_id = lax.broadcasted_iota(jnp.int32, (LANES, gr), 0)
    lane_id = lax.broadcasted_iota(jnp.int32, (LANES, gr), 1)
    spread = jnp.where((copy_id % gr == lane_id) & (copy_id < 3 * gr), 1.0, 0.0).astype(BF16)
    w_copies[1].wait()
    wgb = wgf[...].astype(BF16)
    gap = lax.broadcasted_iota(jnp.int32, (9 * bot, bot), 0) - 9 * lax.broadcasted_iota(jnp.int32, (9 * bot, bot), 1)
    wft[...] = jnp.zeros_like(wft)
    for dh in range(3):
        for dw in range(3):
            pick = jnp.where(gap == 3 * dh + dw, 1.0, 0.0).astype(BF16)
            tap = dot(wgb, pick, 1, 0)
            for c in range(3):
                wft[dh, LANES * dw + gr * c : LANES * dw + gr * (c + 1), :] = tap
            wft[3, LANES * dw + gr * dh : LANES * dw + gr * (dh + 1), :] = tap
    for dh in range(3):
        wfm[dh] = wft[dh].T.astype(BF16)
    wbm[...] = wft[3].astype(BF16)


    tiles_c0, blocks_c0 = lane_tiles(c0), lane_blocks(c0)

    def sums_body(t, carry):
        acc, acc2, count = carry
        pltpu.make_async_copy(x_hbm.at[pl.ds(pl.multiple_of(t * tp, tp), tp)], xv.at[pl.ds(pl.multiple_of(t * tp, tp), tp)], x_sems.at[t]).wait()
        for q in range(TILE_IMGS):
            img = t * TILE_IMGS + q
            is_small = flags[img] > 0
            count = count + jnp.where(is_small, inside_count, 64)
            mask = jnp.where(is_small, inside, 1.0)
            mv[pl.ds(img * 64, 64), :] = jnp.broadcast_to(mask, (64, LANES))
            pmv[pl.ds(img * 16, 16), :] = jnp.broadcast_to(jnp.where(is_small, inside_cell, 1.0), (16, LANES))
        squares, firsts = [], []
        for k, (j, w) in enumerate(tiles_c0):
            total = acc2[k]
            for i in range(0, tp, 32):
                x = xv[pl.ds(pl.multiple_of(t * tp + i, 32), 32), j : j + w].astype(F32)
                total = total + fold_rows(x * x * mv[pl.ds(pl.multiple_of(t * tp + i, 32), 32), 0:w])
            squares.append(total)
        for k, (j, w) in enumerate(blocks_c0):
            cells = dot(pmat[...], xv[pl.ds(pl.multiple_of(t * tp, tp), tp), j : j + w], 1, 0) * pmv[pl.ds(pl.multiple_of(t * tc, tc), tc), 0:1]
            px[pl.ds(pl.multiple_of(t * tc, tc), tc), j : j + w] = cells
            firsts.append(acc[k] + fold_rows(cells))
        return tuple(firsts), tuple(squares), count

    acc, acc2, count = lax.fori_loop(0, tiles, sums_body, (zeros_for(blocks_c0), zeros_for(tiles_c0), jnp.int32(0)))
    acc, acc2 = jnp.concatenate(acc, axis=1), jnp.concatenate(acc2, axis=1)
    red1 = VectorReduce(place, counts, small[0])
    slot = small[0][0]
    span = len(tiles_c0)
    pack_row(slot, r, 0, row_sum(acc))
    pack_row(slot, r, span, row_sum(acc2))
    slot[r, 2 * span : 2 * span + 1, :] = jnp.full((1, LANES), count.astype(F32))
    pl.semaphore_wait(barrier, rows - 1 + batch - 1)
    red1.start()

    w_copies[0].wait()
    w_copies[2].wait()
    wfb[...] = wff[...].astype(BF16)
    wfn[...] = wff[...].T.astype(BF16)
    wlb[...] = wlf[...].astype(BF16)
    red1.middle()
    cot_copies = []
    for step in range(1, rows):
        peer = lax.rem(r + step, rows)
        cot_copies.append(
            pltpu.make_async_remote_copy(
                src_ref=cot_hbm.at[:, pl.ds(pl.multiple_of(peer * 16, 16), 16)],
                dst_ref=cotv.at[pl.ds(r * own, own)],
                send_sem=cot_sems.at[0, step],
                recv_sem=cot_sems.at[1, step],
                device_id={"rows": peer},
                device_id_type=MESH,
            )
        )
    for copy in cot_copies:
        copy.start()

    wlg[...] = dot(spread, wlf[c0:cat, :].astype(BF16), 1, 0).astype(BF16)
    total = red1.finish()
    count_all = total[2 * span : 2 * span + 1, 0:1]
    per = 1.0 / count_all
    mean1 = unpack_row(total, 0, c0) * per
    inv1 = lax.rsqrt(unpack_row(total, span, c0) * per - mean1 * mean1 + EPSILON)
    gain1, shift1 = params[0:1, 0:c0], params[1:2, 0:c0]
    gain2, shift2 = params[0:1, c0 : c0 + bot], params[1:2, c0 : c0 + bot]
    gain3, shift3 = params[0:1, c0 + bot : 2 * c0 + bot], params[1:2, c0 + bot : 2 * c0 + bot]
    gaing, shiftg = params[0:1, 2 * c0 + bot :], params[1:2, 2 * c0 + bot :]
    half_a = 0.5 * gain1 * inv1
    half_b = 0.5 * shift1 - mean1 * half_a
    trans_a = gain3 * inv1
    trans_b = shift3 - mean1 * trans_a
    cvec[0:1, 0:c0] = half_a
    cvec[1:2, 0:c0] = half_b
    cvec[2:3, 0:c0] = 0.25 * trans_a
    cvec[3:4, 0:c0] = trans_b
    cvec[4:5, 0:c0] = mean1
    cvec[5:6, 0:c0] = inv1
    cvec[6:7, 0:c0] = gain1 * inv1
    cvec[7:8, 0:c0] = trans_a

    def first_act(t):
        for j, w in tiles_c0:
            cols = slice(j, j + w)
            scale, shift = cvec[0:1, cols], cvec[1:2, cols]
            for i in range(0, tp, 32):
                at = pl.ds(pl.multiple_of(t * tp + i, 32), 32)
                h = xv[at, cols].astype(F32) * scale + shift
                th = jnp.tanh(h)
                ht = h * th
                av[at, cols] = (h + ht).astype(BF16)
                sv[at, cols] = ((1.0 + th) * (1.0 + (h - ht))).astype(BF16)
            scale, shift = cvec[2:3, cols], cvec[3:4, cols]
            for i in range(0, tc, 32):
                ct = pl.ds(pl.multiple_of(t * tc + i, 32), 32)
                tin[ct, cols] = (px[ct, cols] * scale + pmv[ct, 0:w] * shift).astype(BF16)

    def first_product(t, carry):
        acc, acc2 = carry
        at = pl.ds(pl.multiple_of(t * tp, tp), tp)
        value = dot(av[at, :], wfn[...], 1, 0) * mv[at, 0:1]
        bnv[pl.ds(t * TILE_IMGS, TILE_IMGS)] = value.reshape(TILE_IMGS, 4, 16, bot)
        return acc + fold_rows(value), acc2 + fold_rows(value * value)

    def first_body(t, carry):
        carry = first_product(t - 1, carry)
        first_act(t)
        return carry

    zero = jnp.zeros((8, bot), F32)
    first_act(0)
    acc, acc2 = first_product(tiles - 1, lax.fori_loop(1, tiles, first_body, (zero, zero)))
    red2 = VectorReduce(place, counts, small[1])
    slot = small[1][0]
    pack_row(slot, r, 0, row_sum(acc))
    pack_row(slot, r, 2, row_sum(acc2))
    red2.start()
    a2v[:, 1] = bnv[:, 0].astype(BF16)
    a2v[:, 4] = bnv[:, 3].astype(BF16)

    def edge_copy(ref, sems, side, send):
        return pltpu.make_async_remote_copy(
            src_ref=ref.at[:, 1 + 3 * side],
            dst_ref=ref.at[:, 5 - 5 * side if send else 5 * side],
            send_sem=sems.at[0, side],
            recv_sem=sems.at[1, 1 - side if send else side],
            device_id={"rows": lax.rem(r + rows - 1 + 2 * side, rows)},
            device_id_type=MESH,
        )

    def on_edges(action):
        pl.when(r > 0)(lambda: action(0))
        pl.when(r < rows - 1)(lambda: action(1))

    on_edges(lambda side: edge_copy(a2v, halo_sems, side, True).start())
    cot_own.wait()
    for copy in cot_copies:
        copy.wait()
    red2.middle()

    cot_all = cotv[...].reshape(n_cell, trans)
    eg[...] = dot(cot_all, wlg[...], 1, 1)
    acc_e, acc_ex = [], []
    for j, w in blocks_c0:
        value = dot(cot_all, wlb[j : j + w, :], 1, 1)
        ev[:, j : j + w] = value
        total, total2 = jnp.zeros((8, w), F32), jnp.zeros((8, w), F32)
        for i in range(0, n_cell, 32):
            piece = value[i : i + 32]
            total = total + fold_rows(piece * pmv[i : i + 32, 0:1])
            total2 = total2 + fold_rows(piece * px[i : i + 32, j : j + w])
        acc_e.append(total)
        acc_ex.append(total2)
    acc_e, acc_ex = jnp.concatenate(acc_e, axis=1), jnp.concatenate(acc_ex, axis=1)
    red6 = VectorReduce(place, counts, small[5])
    pack_row(small[5][0], r, 0, row_sum(acc_e))
    pack_row(small[5][0], r, span, row_sum(acc_ex))
    red_a = BlockReduce(place, counts, big[0])
    local_a = big[0][0]
    stride_a = round_up(c0, 16)
    step_rows = 256
    for i in range(0, c0, step_rows):
        n = min(step_rows, c0 - i)
        value = dot(tin[:, i : i + n], cot_all, 0, 0)
        for j in range(0, trans, LANES):
            w = min(LANES, trans - j)
            local_a[j // LANES * stride_a + i : j // LANES * stride_a + i + n, 0:w] = value[:, j : j + w]

    total = red2.finish()
    mean2 = unpack_row(total, 0, bot) * per
    inv2 = lax.rsqrt(unpack_row(total, 2, bot) * per - mean2 * mean2 + EPSILON)
    half_a2 = 0.5 * gain2 * inv2
    half_b2 = 0.5 * shift2 - mean2 * half_a2
    red6.start()
    red_a.start()

    on_edges(lambda side: edge_copy(a2v, halo_sems, side, True).wait_send())

    def middle_body(t, carry):
        imgs = pl.ds(t * TILE_IMGS, TILE_IMGS)
        at = pl.ds(pl.multiple_of(t * tp, tp), tp)
        h = bnv[imgs].reshape(tp, bot) * half_a2 + half_b2
        th = jnp.tanh(h)
        ht = h * th
        mask = mv[at, 0:1]
        a2v[imgs, 1:5] = ((h + ht) * mask).astype(BF16).reshape(TILE_IMGS, 4, 16, bot)
        s2v[at, :] = ((1.0 + th) * (1.0 + (h - ht)) * (0.5 * mask)).astype(BF16)
        return carry

    lax.fori_loop(0, tiles, middle_body, 0)

    on_edges(lambda side: edge_copy(a2v, halo_sems, side, False).wait_recv())
    for side, row, fits, have in ((0, 0, inside_above, have_above), (1, 5, inside_below, have_below)):

        def edge_body(t, carry, side=side, row=row, fits=fits, have=have):
            size = 16
            imgs = pl.ds(pl.multiple_of(t * size, size), size)
            h = a2v[imgs, row].astype(F32).reshape(size * 16, bot) * half_a2 + half_b2
            value = h + h * jnp.tanh(h)
            mask = [jnp.where(flags[t * size + q] > 0, fits, 1.0) * have for q in range(size)]
            value = jnp.where(jnp.concatenate(mask, axis=0) > 0.0, value, 0.0)
            a2v[imgs, row] = value.astype(BF16).reshape(size, 16, bot)
            return carry

        lax.fori_loop(0, images // 16, edge_body, 0)
    red_a.step_b()
    red6.middle()

    col = lax.broadcasted_iota(jnp.int32, (tp, 1), 0) % 16
    not_first, not_last = jnp.where(col > 0, 1.0, 0.0), jnp.where(col < 15, 1.0, 0.0)

    def growth_body(t, carry):
        acc, acc2, acc_e, acc_eg = carry
        imgs = pl.ds(t * TILE_IMGS, TILE_IMGS)
        at, ct = pl.ds(pl.multiple_of(t * tp, tp), tp), pl.ds(pl.multiple_of(t * tc, tc), tc)
        z = dot(a2v[imgs, 0:4].reshape(tp, bot), wfm[0], 1, 0)
        z = z + dot(a2v[imgs, 1:5].reshape(tp, bot), wfm[1], 1, 0)
        z = z + dot(a2v[imgs, 2:6].reshape(tp, bot), wfm[2], 1, 0)
        left = pltpu.roll(z[:, 0:LANES], 1, 0) * not_first
        right = pltpu.roll(z[:, 2 * LANES :], tp - 1, 0) * not_last
        g = left + z[:, LANES : 2 * LANES] + right
        gv[at, :] = g
        gm = g * mv[at, :]
        high, low = split(gm)
        pg = dot(pmat[...], high, 1, 0) + dot(pmat[...], low, 1, 0)
        gt[ct, :] = pg
        e = eg[ct, :]
        return acc + fold_rows(pg), acc2 + fold_rows(gm * g), acc_e + fold_rows(e * pmv[ct, :]), acc_eg + fold_rows(e * pg)

    zero = jnp.zeros((8, LANES), F32)
    sums = lax.fori_loop(0, tiles, growth_body, (zero,) * 4)
    red3 = VectorReduce(place, counts, small[2])
    slot = small[2][0]
    for j in range(4):
        slot[r, j : j + 1, :] = row_sum(sums[j])
    red3.start()

    def part_body(t, carry):
        ct = pl.ds(pl.multiple_of(t * 256, 256), 256)
        px[ct, 0:trans] = dot(tin[ct, :], wlb[0:c0, :], 1, 0)
        return carry

    lax.fori_loop(0, n_cell // 256, part_body, 0)
    red3.middle()
    red_a.step_c()
    poolv[...] = jnp.zeros_like(poolv)
    for c in range(3):
        poolv[0:1, gr * c : gr * (c + 1)] = gaing
        poolv[1:2, gr * c : gr * (c + 1)] = shiftg
    gain_g, shift_g = poolv[0:1, :], poolv[1:2, :]
    total = red3.finish()
    mean_g = total[0:1, :] * per
    inv_g = lax.rsqrt(total[1:2, :] * per - mean_g * mean_g + EPSILON)
    shift_grad_g = total[2:3, :]
    gain_grad_g = inv_g * (0.25 * total[3:4, :] - mean_g * shift_grad_g)
    scale_g = gain_g * inv_g
    slope_g = scale_g * gain_grad_g * inv_g * per
    const_g = slope_g * mean_g - scale_g * shift_grad_g * per
    off_g = shift_g - mean_g * scale_g

    def grad_body(t, carry):
        imgs = pl.ds(t * TILE_IMGS, TILE_IMGS)
        at, ct = pl.ds(pl.multiple_of(t * tp, tp), tp), pl.ds(pl.multiple_of(t * tc, tc), tc)
        high, low = split(eg[ct, :] * (0.25 * scale_g) + const_g)
        wide = dot(umat[...], high, 1, 0) + dot(umat[...], low, 1, 0)
        gg = (wide - gv[at, :] * slope_g) * mv[at, :]
        ggv[imgs, 1:5] = gg.astype(BF16).reshape(TILE_IMGS, 4, 16, LANES)
        ting[ct, :] = (gt[ct, :] * (0.25 * scale_g) + pmv[ct, :] * off_g).astype(BF16)
        return carry

    lax.fori_loop(0, tiles, grad_body, 0)

    on_edges(lambda side: edge_copy(ggv, gg_sems, side, True).start())

    @pl.when(r == 0)
    def _():
        ggv[:, 0] = jnp.zeros((images, 16, LANES), BF16)

    @pl.when(r == rows - 1)
    def _():
        ggv[:, 5] = jnp.zeros((images, 16, LANES), BF16)

    lane = lax.broadcasted_iota(jnp.int32, (1, LANES), 1)

    def pool_body(t, carry):
        ct = pl.ds(pl.multiple_of(t * 256, 256), 256)
        own_g = jnp.where(lane < gr, ting[ct, :].astype(F32), 0.0).astype(BF16)
        value = px[ct, 0:trans] + dot(own_g, wlg[...], 1, 0)
        hpool[pl.ds(t * 16, 16)] = value.astype(BF16).reshape(16, 16, trans)
        return carry

    hpool = take(1)[0]
    lax.fori_loop(0, n_cell // 256, pool_body, 0)
    pool_copies = []
    for step in range(1, rows):
        peer = lax.rem(r + step, rows)
        pool_copies.append(
            pltpu.make_async_remote_copy(
                src_ref=hpool.at[pl.ds(peer * own, own)],
                dst_ref=pool_hbm.at[:, pl.ds(pl.multiple_of(r * 16, 16), 16)],
                send_sem=pool_sems.at[0, step],
                recv_sem=pool_sems.at[1, step],
                device_id={"rows": peer},
                device_id_type=MESH,
            )
        )
    red_a.step_d()
    red_c = BlockReduce(place, counts, big[1])
    local_c[...] = jnp.zeros_like(local_c)
    base_c = len(tiles_c0) * round_up(bot, 8)
    stride_g = round_up(gr, 8)
    value = dot(ting[...], cot_all, 0, 0)
    for j in range(0, trans, LANES):
        w = min(LANES, trans - j)
        top = base_c + j // LANES * stride_g
        local_c[top : top + gr, 0:w] = value[0:gr, j : j + w]
    base_taps = base_c + -(-trans // LANES) * stride_g

    on_edges(lambda side: edge_copy(ggv, gg_sems, side, True).wait_send())
    on_edges(lambda side: edge_copy(ggv, gg_sems, side, False).wait_recv())
    lanes_all = lax.broadcasted_iota(jnp.int32, (tp, LANES), 1)
    wft[0] = jnp.zeros(wft.shape[1:], F32)

    def conv_body(t, carry):
        acc, acc2 = carry
        imgs = pl.ds(t * TILE_IMGS, TILE_IMGS)
        at = pl.ds(pl.multiple_of(t * tp, tp), tp)
        above = ggv[imgs, 0:4].reshape(tp, LANES).astype(F32)
        here = ggv[imgs, 1:5].reshape(tp, LANES).astype(F32)
        below = ggv[imgs, 2:6].reshape(tp, LANES).astype(F32)
        mixed = jnp.where(lanes_all < gr, below, jnp.where(lanes_all < 2 * gr, here, jnp.where(lanes_all < 3 * gr, above, 0.0)))
        from_right = pltpu.roll(mixed, tp - 1, 0) * not_last
        from_left = pltpu.roll(mixed, 1, 0) * not_first
        patch = jnp.concatenate([from_right, mixed, from_left], axis=1).astype(BF16)
        gm = dot(patch, wbm[...], 1, 0) * s2v[at, :].astype(F32)
        gmv[at, :] = gm
        wft[0] += dot(patch, a2v[imgs, 1:5].reshape(tp, bot), 0, 0)
        hat = bnv[imgs].reshape(tp, bot) - mean2
        return acc + fold_rows(gm), acc2 + fold_rows(gm * hat)

    zero = jnp.zeros((8, bot), F32)
    acc, acc2 = lax.fori_loop(0, tiles, conv_body, (zero, zero))
    red4 = VectorReduce(place, counts, small[3])
    slot = small[3][0]
    pack_row(slot, r, 0, row_sum(acc))
    pack_row(slot, r, 2, row_sum(acc2))
    red4.start()
    red4.middle()
    red_a.step_e()
    gap = lax.broadcasted_iota(jnp.int32, (bot, 9 * bot), 1) - 9 * lax.broadcasted_iota(jnp.int32, (bot, 9 * bot), 0)
    value = jnp.zeros((gr, 9 * bot), F32)
    for dh in range(3):
        for dw in range(3):
            pick = jnp.where(gap == 3 * dh + dw, 1.0, 0.0).astype(BF16)
            tap = wft[0, LANES * dw + gr * dh : LANES * dw + gr * (dh + 1), :]
            high, low = split(tap)
            value = value + (dot(high, pick, 1, 0) + dot(low, pick, 1, 0))
    for j in range(0, 9 * bot, LANES):
        w = min(LANES, 9 * bot - j)
        top = base_taps + j // LANES * stride_g
        local_c[top : top + gr, 0:w] = value[:, j : j + w]
    total = red4.finish()
    shift_grad2 = unpack_row(total, 0, bot)
    gain_grad2 = inv2 * unpack_row(total, 2, bot)
    scale2 = gain2 * inv2
    slope2 = scale2 * gain_grad2 * inv2 * per
    const2 = scale2 * shift_grad2 * per - slope2 * mean2
    for copy in pool_copies:
        copy.start()
    pool_own = pltpu.make_async_copy(
        hpool.at[pl.ds(r * own, own)], pool_hbm.at[:, pl.ds(pl.multiple_of(r * 16, 16), 16)], io_sems.at[4]
    )
    pool_own.start()

    stride_f = round_up(bot, 8)
    blocks = -(-c0 // LANES)

    def bottleneck_body(t, carry):
        imgs = pl.ds(t * TILE_IMGS, TILE_IMGS)
        at = pl.ds(pl.multiple_of(t * tp, tp), tp)
        bn = bnv[imgs].reshape(tp, bot)
        gb = ((gmv[at, :] * scale2 - bn * slope2 - const2) * mv[at, 0:1]).astype(BF16)
        s2v[at, :] = gb
        grad = dot(gb, av[at, :], 0, 0)
        for k, (j, w) in enumerate(tiles_c0):
            local_b[k * stride_f : k * stride_f + bot, 0:w] += grad[:, j : j + w]
        return carry

    lax.fori_loop(0, tiles, bottleneck_body, 0)
    red_c.start()

    def back_body(t, carry):
        acc, acc2 = carry
        at = pl.ds(pl.multiple_of(t * tp, tp), tp)
        gb = s2v[at, :]
        sums, cross = [], []
        for k, (j, w) in enumerate(blocks_c0):
            cols = slice(j, j + w)
            value = dot(gb, wfb[:, cols], 1, 0)
            total, total2 = acc[k], acc2[k]
            for i in range(0, tp, 32):
                part = pl.ds(pl.multiple_of(t * tp + i, 32), 32)
                gf = value[i : i + 32] * sv[part, cols].astype(F32)
                av[part, cols] = gf.astype(BF16)
                total = total + fold_rows(gf)
                total2 = total2 + fold_rows(gf * xv[part, cols].astype(F32))
            sums.append(total)
            cross.append(total2)
        return tuple(sums), tuple(cross)

    zero = zeros_for(blocks_c0)
    sums = lax.fori_loop(0, tiles // 2, back_body, (zero, zero))
    red_c.step_b()
    sums = lax.fori_loop(tiles // 2, tiles, back_body, sums)
    acc, acc2 = jnp.concatenate(sums[0], axis=1), jnp.concatenate(sums[1], axis=1)
    red5 = VectorReduce(place, counts, small[4])
    pack_row(small[4][0], r, 0, row_sum(acc))
    pack_row(small[4][0], r, span, row_sum(acc2))
    red5.start()
    red_c.step_c()
    cvec[0:1, 0:c0] = 0.25 * cvec[7:8, 0:c0]
    cvec[2:3, 0:c0] = 0.5 * cvec[6:7, 0:c0]

    def part_grad(t, carry):
        for q in range(TILE_IMGS):
            img = t * TILE_IMGS + q
            for j, w in tiles_c0:
                cols, full = slice(j, j + w), slice(j, j + LANES)
                ct = pl.ds(pl.multiple_of(img * 16, 16), 16)
                cells = ev[ct, full] * cvec[0:1, full] * pmv[ct, :]
                up[j // LANES, pl.ds(0, 16, stride=2), :] = cells
                up[j // LANES, pl.ds(1, 16, stride=2), :] = cells
                scale = cvec[2:3, cols]
                for half in range(2):
                    at = pl.ds(pl.multiple_of(img * 64 + half * 32, 32), 32)
                    wide_cells = up[j // LANES, half * 16 : half * 16 + 16, 0:w]
                    wide_cells = jnp.concatenate([wide_cells, wide_cells], axis=0)
                    sv[at, cols] = (wide_cells + av[at, cols].astype(F32) * scale).astype(BF16)
        return carry

    lax.fori_loop(0, tiles // 4, part_grad, 0)
    red5.middle()
    lax.fori_loop(tiles // 4, 7 * tiles // 12, part_grad, 0)
    red_c.step_d()
    lax.fori_loop(7 * tiles // 12, tiles, part_grad, 0)
    red_a.step_f()
    total = red5.finish()
    red_c.step_e()
    mean1, inv1 = cvec[4:5, 0:c0], cvec[5:6, 0:c0]
    scale1, scale3 = cvec[6:7, 0:c0], cvec[7:8, 0:c0]
    shift_grad1 = 0.5 * unpack_row(total, 0, c0)
    gain_grad1 = inv1 * (0.5 * unpack_row(total, span, c0) - mean1 * shift_grad1)
    total = red6.finish()
    shift_grad3 = unpack_row(total, 0, c0)
    gain_grad3 = inv1 * (0.25 * unpack_row(total, span, c0) - mean1 * shift_grad3)
    slope1 = (scale3 * gain_grad3 + scale1 * gain_grad1) * inv1 * per
    const1 = (scale3 * shift_grad3 + scale1 * shift_grad1) * per - slope1 * mean1
    stats[...] = jnp.zeros_like(stats)
    stats[0:1, 0:c0] = gain_grad1
    stats[1:2, 0:c0] = shift_grad1
    stats[2:3, 0:bot] = gain_grad2
    stats[3:4, 0:bot] = shift_grad2
    stats[4:5, 0:c0] = gain_grad3
    stats[5:6, 0:c0] = shift_grad3
    stats[6:7, 0:LANES] = gain_grad_g
    stats[7:8, 0:LANES] = shift_grad_g
    stats[8:9, :] = jnp.broadcast_to(count_all, (1, stats.shape[1]))
    cvec[1:2, 0:c0] = const1
    cvec[3:4, 0:c0] = slope1

    def out_copy(t):
        at = pl.ds(pl.multiple_of(t * tp, tp), tp)
        return pltpu.make_async_copy(av.at[at], ig_hbm.at[at], x_sems.at[t])

    def last_body(t, carry):
        for q in range(TILE_IMGS):
            img = t * TILE_IMGS + q
            for j, w in tiles_c0:
                cols = slice(j, j + w)
                slope, const = cvec[3:4, cols], cvec[1:2, cols]
                for i in range(0, 64, 32):
                    at = pl.ds(pl.multiple_of(img * 64 + i, 32), 32)
                    value = (xv[at, cols].astype(F32) * slope + const) * mv[at, 0:w]
                    av[at, cols] = (sv[at, cols].astype(F32) - value).astype(BF16)
        out_copy(t).start()
        return carry

    lax.fori_loop(0, tiles // 2, last_body, 0)
    red_c.step_f()
    lax.fori_loop(tiles // 2, tiles, last_body, 0)
    red_a.finish()
    out_a = pltpu.make_async_copy(big[0][5], sum_a, io_sems.at[0])
    out_a.start()
    red_c.finish()
    out_c = pltpu.make_async_copy(big[1][5], sum_c, io_sems.at[2])
    out_c.start()
    pool_own.wait()
    for copy in pool_copies:
        copy.wait()
    for t in range(tiles):
        out_copy(t).wait()
    out_a.wait()
    out_c.wait()


def mm3(a, b, ca, cb):
    left = jnp.concatenate([a[0], a[0], a[1]], axis=ca)
    right = jnp.concatenate([b[0], b[1], b[0]], axis=cb)
    return dot(left, right, ca, cb)


def orthogonal_steps(pads, sides, sizes, found):
    start, gram, prod, ones = [], [], [], []
    for pad, side, size in zip(pads, sides, sizes):
        halves = unit_norm(pad)
        start.append(halves)
        gram.append(mm3(halves, halves, side, side))
        full = gram[-1].shape[0]
        i, j = (lax.broadcasted_iota(jnp.int32, (full, full), d) for d in (0, 1))
        ones.append((i == j) & (i < size))
        prod.append(None)
    yield
    for k in range(NS_STEPS):
        halves = [split(g) for g in gram]
        square = [mm3(h, h, 1, 0) for h in halves]
        poly = [jnp.where(o, QUINTIC_A, 0.0) + QUINTIC_B * g + QUINTIC_C * s for o, g, s in zip(ones, gram, square)]
        poly_h = [split(p) for p in poly]
        if k < NS_STEPS - 1:
            mid = [split(mm3(h, p, 1, 0)) for h, p in zip(halves, poly_h)]
            gram = [mm3(m, p, 1, 0) for m, p in zip(mid, poly_h)]
        prod = [p if k == 0 else split(mm3(q, p, 1, 0)) for q, p in zip(prod, poly_h)]
        if k == NS_STEPS - 1:
            found.extend(zip(start, prod))
        yield


def unit_norm(pad):
    value = pad[...]
    norm = jnp.sqrt(jnp.sum(jnp.sum(value * value, axis=0, keepdims=True), axis=1, keepdims=True)) + TINY
    pad[...] = value / norm
    return split(pad[...])


class LoopedOrthogonal:
    def __init__(self, valid, refs):
        self.valid = valid
        self.stack, self.poly, self.mid = refs
        self.full = self.poly.shape[1]

    @staticmethod
    def scratch(full):
        return [pltpu.VMEM((2, 2 * full, full), BF16), pltpu.VMEM((2, full, full), BF16), pltpu.VMEM((2, full, full), BF16)]

    def store(self, ref, start, value):
        high, low = split(value)
        ref[0, start : start + value.shape[0]] = high
        ref[1, start : start + value.shape[0]] = low

    def unit(self, scale):
        i, j = (lax.broadcasted_iota(jnp.int32, (self.full, self.full), d) for d in (0, 1))
        return jnp.where((i == j) & self.valid(i), scale, 0.0)

    def begin(self, gram):
        self.store(self.stack, 0, gram)
        self.stack[0, self.full :] = self.unit(1.0).astype(BF16)
        self.stack[1, self.full :] = jnp.zeros((self.full, self.full), BF16)

    def polynomial(self):
        n = self.full
        high, low = self.stack[0, 0:n], self.stack[1, 0:n]
        square = mm3((high, low), (high, low), 1, 0)
        gram = high.astype(F32) + low.astype(F32)
        self.store(self.poly, 0, self.unit(QUINTIC_A) + QUINTIC_B * gram + QUINTIC_C * square)

    def step(self, k, carry):
        n = self.full
        self.polynomial()
        poly = (self.poly[0], self.poly[1])
        both = mm3((self.stack[0], self.stack[1]), poly, 1, 0)
        self.store(self.mid, 0, both[0:n])
        self.store(self.stack, n, both[n:])
        self.store(self.stack, 0, mm3((self.mid[0], self.mid[1]), poly, 1, 0))
        return carry

    def light_step(self, k, carry):
        n = self.full
        high = self.stack[0, 0:n]
        gram = high.astype(F32) + self.stack[1, 0:n].astype(F32)
        poly = (QUINTIC_B * gram + QUINTIC_C * dot(high, high, 1, 0)).astype(BF16)
        self.poly[0] = poly
        both = self.stack[0].astype(F32) + self.stack[1].astype(F32)
        both = QUINTIC_A * both + dot(self.stack[0], poly, 1, 0)
        self.store(self.stack, n, both[n:])
        mid = both[0:n]
        self.store(self.stack, 0, QUINTIC_A * mid + dot(mid.astype(BF16), self.poly[0], 1, 0))
        return carry

    def finish(self):
        n = self.full
        self.polynomial()
        return split(mm3((self.stack[0, n:], self.stack[1, n:]), (self.poly[0], self.poly[1]), 1, 0))


def sum_rows(ref, top, count, width):
    base = top // 16 * 16
    size = min(round_up(top - base + count, 16), ref.shape[0] - base)
    return ref[base : base + size, :].astype(F32)[top - base : top - base + count, 0:width]


def transition_moment(c0, gr, trans, ml, sum_a, sum_c, base, put):
    stride_a, stride_g = round_up(c0, 16), round_up(gr, 8)
    for j, w in lane_tiles(trans):
        k = j // LANES
        put(slice(0, c0), slice(j, j + w), MOMENTUM_DECAY * ml[0:c0, j : j + w] + sum_rows(sum_a, k * stride_a, c0, w))
        rows = slice(c0, c0 + gr)
        put(rows, slice(j, j + w), MOMENTUM_DECAY * ml[rows, j : j + w] + sum_rows(sum_c, base + k * stride_g, gr, w))


def update_kernel(dims, ig_in, pool_in, wl_hbm, ml_hbm, stats, sum_a, sum_c, params, p_moment, wf, wg, mf, mg, *refs):
    (c0, bot, gr, trans) = dims
    cat = c0 + gr
    (ig_out, pool_out, wl_out, ml_out, p_moment_new, params_new, mf_new, mg_new, wf_new, wg_new) = refs[:10]
    (lpad, spad, igv, poolv, wl, ml, sems) = refs[10:17]
    low = round_up(bot, 8)
    loops = [
        LoopedOrthogonal(lambda i: i < trans, refs[17:20]),
        LoopedOrthogonal(lambda i: (i < bot) | ((i >= low) & (i < low + gr)), refs[20:23]),
    ]
    loads = [pltpu.make_async_copy(ml_hbm, ml, sems.at[0, 0]), pltpu.make_async_copy(wl_hbm, wl, sems.at[0, 1])]
    loads += [pltpu.make_async_copy(ig_in, igv, sems.at[0, 2]), pltpu.make_async_copy(pool_in, poolv, sems.at[0, 3])]
    stores = [pltpu.make_async_copy(ml, ml_out, sems.at[1, 0]), pltpu.make_async_copy(wl, wl_out, sems.at[1, 1])]
    stores += [pltpu.make_async_copy(igv, ig_out, sems.at[1, 2]), pltpu.make_async_copy(poolv, pool_out, sems.at[1, 3])]
    for copy in loads:
        copy.start()

    count = stats[8:9, 0:1]
    step = NORM_RATE * lax.rsqrt(count)
    spans = ((0, c0, 0), (c0, bot, 2), (c0 + bot, c0, 4), (2 * c0 + bot, gr, 6))
    for start, width, row in spans:
        moment = MOMENTUM_DECAY * p_moment[:, start : start + width] + stats[row : row + 2, 0:width]
        p_moment_new[:, start : start + width] = moment
        params_new[:, start : start + width] = params[:, start : start + width] - step * moment

    stride_g, stride_f = round_up(gr, 8), round_up(bot, 8)
    lpad[...] = jnp.zeros_like(lpad)
    spad[...] = jnp.zeros_like(spad)
    base = len(lane_tiles(c0)) * stride_f
    for j, w in lane_tiles(c0):
        new = MOMENTUM_DECAY * mf[:, j : j + w] + sum_rows(sum_c, j // LANES * stride_f, bot, w)
        mf_new[:, j : j + w] = new
        spad[0:bot, j : j + w] = new
    loads[0].wait()

    def put(at, cols, value):
        ml[at, cols] = value
        lpad[at, cols] = value

    transition_moment(c0, gr, trans, ml, sum_a, sum_c, base, put)
    stores[0].start()
    base = base + len(lane_tiles(trans)) * stride_g
    for j, w in lane_tiles(9 * bot):
        new = MOMENTUM_DECAY * mg[:, j : j + w] + sum_rows(sum_c, base + j // LANES * stride_g, gr, w)
        mg_new[:, j : j + w] = new
        spad[low : low + gr, j : j + w] = new
    halves = unit_norm(lpad)
    loops[0].begin(mm3(halves, halves, 0, 0))
    norms = []
    for start, stop in ((0, low), (low, low + round_up(gr, 8))):
        value = spad[start:stop, :]
        total = jnp.sum(jnp.sum(value * value, axis=0, keepdims=True), axis=1, keepdims=True)
        norms.append(1.0 / (jnp.sqrt(total) + TINY))
    row = lax.broadcasted_iota(jnp.int32, (spad.shape[0], 1), 0)
    spad[...] = spad[...] * jnp.where(row < low, norms[0], norms[1])
    halves = split(spad[...])
    gram = mm3(halves, halves, 1, 1)
    i, j = (lax.broadcasted_iota(jnp.int32, gram.shape, d) for d in (0, 1))
    loops[1].begin(jnp.where((i < low) == (j < low), gram, 0.0))
    for k in (2, 3):
        loads[k].wait()
        stores[k].start()

    def light(k, carry):
        loops[0].light_step(k, carry)
        loops[1].step(k, carry)
        return carry

    def full(k, carry):
        for loop in loops:
            loop.step(k, carry)
        return carry

    lax.fori_loop(0, 2, light, 0)
    lax.fori_loop(2, 4, full, 0)
    prods = [loop.finish() for loop in loops]
    ortho = mm3(split(lpad[...]), prods[0], 1, 0)
    loads[1].wait()
    wl[...] = wl[...] - MUON_RATE * ortho[0:cat, 0:trans]
    stores[1].start()
    ortho = mm3(prods[1], split(spad[...]), 1, 0)
    wf_new[...] = wf[...] - MUON_RATE * ortho[0:bot, 0:c0]
    wg_new[...] = wg[...] - MUON_RATE * ortho[low : low + gr, 0 : 9 * bot]
    for copy in stores:
        copy.wait()


def per_device(counts, inputs, small_flags, norm_params, norm_moment, w_bottleneck, w_growth, w_transition,
               m_bottleneck, m_growth, m_transition, cotangent):
    rows, batch = counts
    images, band, width, c0 = inputs.shape
    bot, gr, trans = w_bottleneck.shape[1], w_growth.shape[1], w_transition.shape[1]
    own = cotangent.shape[0]
    cat = c0 + gr
    n_pix, n_cell = images * 64, images * 16
    assert rows == 4 and band == 4 and width == 16 and images % 16 == 0
    any_spec = pl.BlockSpec(memory_space=pl.ANY)
    vmem_spec = pl.BlockSpec(memory_space=pltpu.VMEM)
    smem_spec = pl.BlockSpec(memory_space=pltpu.SMEM)
    wide = round_up(c0, LANES)
    unit = 16 * 4 * batch
    blocks = -(-trans // LANES)
    rows_b = -(-c0 // LANES) * round_up(bot, 8)
    rows_c = (blocks + -(-9 * bot // LANES)) * round_up(gr, 8)
    length_a = round_up(blocks * round_up(c0, 16), unit)
    length_c = round_up(rows_b + rows_c, unit)
    dims = (rows, batch, images, c0, bot, gr, trans, own)
    v = pltpu.VMEM
    dma = pltpu.SemaphoreType.DMA

    def vector_scratch(height):
        return [v((rows, height, LANES), F32), v((batch, height, LANES), F32), dma((2, rows)), dma((2, batch))]

    scratch = [
        v((n_pix, c0), BF16), v((n_pix, c0), BF16), v((n_pix, c0), BF16),
        v((n_pix, LANES), F32), v((n_cell, LANES), F32),
        v((n_cell, c0), F32), v((n_cell, c0), BF16), v((n_cell, LANES), BF16),
        v((n_cell, wide), F32), v((n_cell, LANES), F32), v((images, 16, trans), BF16),
        v((images, 4, 16, bot), F32),
        v((images, 6, 16, bot), BF16), v((n_pix, bot), BF16), v((n_pix, LANES), F32),
        v((images, 6, 16, LANES), BF16), v((n_pix, bot), F32),
        v((cat, trans), F32), v((cat, trans), BF16), v((LANES, trans), BF16),
        v((bot, c0), F32), v((bot, c0), BF16), v((c0, bot), BF16), v((gr, 9 * bot), F32),
        v((4, 3 * LANES, bot), F32), v((3, bot, 3 * LANES), BF16), v((3 * LANES, bot), BF16),
        v((TILE_IMGS * 16, TILE_IMGS * 64), BF16), v((TILE_IMGS * 64, TILE_IMGS * 16), BF16),
        v((8, wide), F32), v((8, LANES), F32), v((n_cell, LANES), F32),
        dma((images // TILE_IMGS,)), dma((5,)), dma((2, rows)), dma((2, 2)), dma((2, 2)), dma((2, rows)),
    ]
    for height in (16, 8, 8, 8):
        scratch += vector_scratch(height)
    scratch += [dma((2, rows)), dma((2, batch))] + vector_scratch(16)
    for length in (length_a, length_c):
        scratch += BlockReduce.scratch(length, batch)
    scratch += [v((wide // LANES, 32, LANES), F32)]
    scratch += [v((images, 16, trans), BF16)]
    struct = jax.ShapeDtypeStruct
    input_grad, pooled, stats, sum_a, sum_c = pl.pallas_call(
        functools.partial(band_kernel, dims),
        out_shape=(
            struct((n_pix, c0), BF16),
            struct((own, 64, trans), BF16),
            struct((16, wide), F32),
            struct((length_a, LANES), BF16),
            struct((length_c, LANES), BF16),
        ),
        in_specs=[smem_spec, any_spec, any_spec, vmem_spec, any_spec, any_spec, any_spec],
        out_specs=[any_spec, any_spec, vmem_spec, any_spec, any_spec],
        scratch_shapes=scratch,
        compiler_params=pltpu.CompilerParams(collective_id=0, has_side_effects=True, vmem_limit_bytes=VMEM_BYTES),
        name="band",
    )(
        small_flags,
        inputs.reshape(n_pix, c0),
        cotangent.reshape(own, 64, trans),
        norm_params,
        w_bottleneck.T,
        w_growth.T,
        w_transition,
    )
    vectors = [struct(norm_params.shape, F32)] * 2
    weights = [struct((bot, c0), F32), struct((gr, 9 * bot), F32)]
    outs = pl.pallas_call(
        functools.partial(update_kernel, (c0, bot, gr, trans)),
        out_shape=[struct((n_pix, c0), BF16), struct((own, 64, trans), BF16)]
        + [struct((cat, trans), F32)] * 2
        + vectors
        + weights * 2,
        in_specs=[any_spec] * 4 + [vmem_spec] * 9,
        out_specs=[any_spec] * 4 + [vmem_spec] * 6,
        scratch_shapes=[
            v((round_up(cat, 128), 4 * LANES), F32),
            v((round_up(bot + gr + 16, 256), round_up(max(c0, 9 * bot), LANES)), F32),
            v((n_pix, c0), BF16),
            v((own, 64, trans), BF16),
            v((cat, trans), F32),
            v((cat, trans), F32),
            dma((2, 4)),
        ]
        + LoopedOrthogonal.scratch(4 * LANES)
        + LoopedOrthogonal.scratch(round_up(bot + gr + 16, 256)),
        compiler_params=pltpu.CompilerParams(vmem_limit_bytes=VMEM_BYTES),
        name="update",
    )(
        input_grad, pooled, w_transition, m_transition, stats, sum_a, sum_c, norm_params, norm_moment, w_bottleneck.T,
        w_growth.T, m_bottleneck.T, m_growth.T,
    )
    (ig, pooled, wl_new, ml_new, moment_new, params_new, mf_new, mg_new, wf_new, wg_new) = outs
    return (
        pooled.reshape(cotangent.shape),
        ig.reshape(inputs.shape),
        moment_new,
        params_new,
        mf_new.T,
        mg_new.T,
        ml_new,
        wf_new.T,
        wg_new.T,
        wl_new,
    )


def solution(mesh):
    counts = (mesh.shape["rows"], mesh.shape["batch"])
    whole = (P(),) * 8
    images = P(("batch", "rows"), None, None, None)
    bands = P("batch", "rows", None, None)
    return jax.shard_map(
        functools.partial(per_device, counts),
        mesh=mesh,
        in_specs=(bands, P("batch")) + whole + (images,),
        out_specs=(images, bands) + whole,
        check_vma=False,
    )
```

```python
import functools

import jax
import jax.numpy as jnp
from jax import lax
from jax.experimental import pallas as pl
from jax.experimental.pallas import tpu as pltpu
from jax.sharding import PartitionSpec as P

SMALL = 12
NS_STEPS = 5
EPSILON = 1e-05
MOMENTUM_DECAY = 0.9
MUON_RATE = 0.5
NORM_RATE = 1.0
QUINTIC_A = 3.4445
QUINTIC_B = -4.775
QUINTIC_C = 2.0315
TINY = 1e-07
F32 = jnp.float32
BF16 = jnp.bfloat16
MESH = pl.DeviceIdType.MESH
LANES = 128
TILE_IMGS = 8
VMEM_BYTES = 62 * 1024 * 1024


def dot(a, b, ca, cb):
    return lax.dot_general(a, b, (((ca,), (cb,)), ((), ())), preferred_element_type=F32)


def split(a):
    high = a.astype(BF16)
    return high, (a - high.astype(F32)).astype(BF16)


def round_up(value, step):
    return -(-value // step) * step


def fold_rows(value):
    rows, cols = value.shape
    return jnp.sum(value.reshape(rows // 8, 8, cols), axis=0)


def lane_tiles(total):
    return [(j, min(LANES, total - j)) for j in range(0, total, LANES)]


def lane_blocks(total):
    return [(j, min(2 * LANES, total - j)) for j in range(0, total, 2 * LANES)]


def zeros_for(pieces):
    return tuple(jnp.zeros((8, w), F32) for _, w in pieces)


def pack_row(slots, r, top, row):
    for k, (j, w) in enumerate(lane_tiles(row.shape[1])):
        slots[r, top + k : top + k + 1, 0:w] = row[:, j : j + w]


def unpack_row(total, top, size):
    return jnp.concatenate([total[top + k : top + k + 1, 0:w] for k, (_, w) in enumerate(lane_tiles(size))], axis=1)


def row_sum(value):
    return jnp.sum(value, axis=0, keepdims=True)


class VectorReduce:
    def __init__(self, place, counts, refs):
        self.r, self.b = place
        self.rows, self.batch = counts
        self.row_slots, self.batch_slots, self.row_sems, self.batch_sems = refs

    def copies(self, axis, me, count, slots, sems):
        made = []
        for step in range(1, count):
            peer = lax.rem(me + step, count)
            made.append(
                pltpu.make_async_remote_copy(
                    src_ref=slots.at[me],
                    dst_ref=slots.at[me],
                    send_sem=sems.at[0, step],
                    recv_sem=sems.at[1, step],
                    device_id={axis: peer},
                    device_id_type=MESH,
                )
            )
        return made

    def start(self):
        self.first = self.copies("rows", self.r, self.rows, self.row_slots, self.row_sems)
        for copy in self.first:
            copy.start()

    def middle(self):
        for copy in self.first:
            copy.wait_recv()
        total = self.row_slots[0]
        for j in range(1, self.rows):
            total = total + self.row_slots[j]
        self.batch_slots[self.b] = total
        self.second = self.copies("batch", self.b, self.batch, self.batch_slots, self.batch_sems)
        for copy in self.second:
            copy.start()

    def finish(self):
        for copy in self.second:
            copy.wait_recv()
        total = self.batch_slots[0]
        for j in range(1, self.batch):
            total = total + self.batch_slots[j]
        for copy in self.first + self.second:
            copy.wait_send()
        return total


class BlockReduce:
    def __init__(self, place, counts, refs):
        self.r, self.b = place
        self.batch = counts[1]
        self.local, self.out_a, self.in_a, self.in_b, self.in_c, self.full, self.sems = refs
        self.length = self.local.shape[0]
        self.out_b = self.out_a.at[pl.ds(0, self.length // 4)]
        self.out_c = self.out_a.at[pl.ds(self.length // 4, self.length // 4)]
        self.chunk = self.length // (4 * self.batch)
        self.low, self.high = lax.rem(self.r, 2), lax.div(self.r, 2)
        self.near = self.r + 1 - 2 * self.low
        self.far = self.r + 2 - 4 * self.high

    def each(self, count, body):
        step = 16
        for size in (256, 128, 64, 32):
            if count % size == 0:
                step = size
                break

        def run(i, carry):
            body(pl.multiple_of(i * step, 16), step)
            return carry

        lax.fori_loop(0, count // step, run, 0)

    def copy(self, src, dst, axis, peer, slot):
        return pltpu.make_async_remote_copy(
            src_ref=src,
            dst_ref=dst,
            send_sem=self.sems.at[0, slot],
            recv_sem=self.sems.at[1, slot],
            device_id={axis: peer},
            device_id_type=MESH,
        )

    def at(self, start, size):
        return pl.ds(pl.multiple_of(start, 16), size)

    def start(self):
        half = self.length // 2
        other = (1 - self.low) * half

        def body(i, n):
            self.out_a[self.at(i, n)] = self.local[self.at(other + i, n)].astype(BF16)

        self.each(half, body)
        self.a = self.copy(self.out_a, self.in_a, "rows", self.near, 0)
        self.a.start()

    def step_b(self):
        quarter = self.length // 4
        self.a.wait()
        other = (1 - self.high) * quarter
        mine = self.low * 2 * quarter

        def body(i, n):
            total = self.local[self.at(mine + other + i, n)] + self.in_a[self.at(other + i, n)].astype(F32)
            self.out_b[self.at(i, n)] = total.astype(BF16)

        self.each(quarter, body)
        self.b_copy = self.copy(self.out_b, self.in_b, "rows", self.far, 1)
        self.b_copy.start()

    def step_c(self):
        quarter = self.length // 4
        self.b_copy.wait()
        mine = self.low * 2 * quarter + self.high * quarter

        def body(i, n):
            total = self.local[self.at(mine + i, n)] + self.in_a[self.at(self.high * quarter + i, n)].astype(F32)
            total = total + self.in_b[self.at(i, n)].astype(F32)
            self.local[self.at(mine + i, n)] = total
            self.out_c[self.at(i, n)] = total.astype(BF16)

        self.each(quarter, body)
        self.c = []
        for step in range(1, self.batch):
            peer = lax.rem(self.b + step, self.batch)
            piece = self.out_c.at[self.at(peer * self.chunk, self.chunk)]
            self.c.append(self.copy(piece, self.in_c.at[step], "batch", peer, 1 + step))
        for copy in self.c:
            copy.start()

    def step_d(self):
        quarter = self.length // 4
        for copy in self.c:
            copy.wait()
        mine = self.low * 2 * quarter + self.high * quarter + self.b * self.chunk

        def body(i, n):
            total = self.local[self.at(mine + i, n)]
            for step in range(1, self.batch):
                total = total + self.in_c[step, self.at(i, n)].astype(F32)
            self.full[self.at(mine + i, n)] = total.astype(BF16)

        self.each(self.chunk, body)
        piece = self.full.at[self.at(mine, self.chunk)]
        self.d = []
        for step in range(1, self.batch):
            peer = lax.rem(self.b + step, self.batch)
            self.d.append(self.copy(piece, piece, "batch", peer, self.batch + step))
        for copy in self.d:
            copy.start()

    def step_e(self):
        quarter = self.length // 4
        for copy in self.d:
            copy.wait()
        self.e_copy().start()

    def e_copy(self):
        quarter = self.length // 4
        piece = self.full.at[self.at(self.low * 2 * quarter + self.high * quarter, quarter)]
        return self.copy(piece, piece, "rows", self.far, 2 * self.batch)

    def step_f(self):
        half = self.length // 2
        self.e_copy().wait()
        piece = self.full.at[self.at(self.low * half, half)]
        self.f = self.copy(piece, piece, "rows", self.near, 2 * self.batch + 1)
        self.f.start()

    def finish(self):
        self.f.wait()

    @staticmethod
    def scratch(length, batch):
        shapes = (length // 2, length // 2, length // 4)
        return (
            [pltpu.VMEM((length, LANES), F32)]
            + [pltpu.VMEM((n, LANES), BF16) for n in shapes]
            + [
                pltpu.VMEM((batch, length // (4 * batch), LANES), BF16),
                pltpu.VMEM((length, LANES), BF16),
                pltpu.SemaphoreType.DMA((2, 2 * batch + 2)),
            ]
        )


def band_kernel(dims, flags, x_hbm, cot_hbm, params, wf_hbm, wg_hbm, wl_hbm, *rest):
    (rows, batch, images, c0, bot, gr, trans, own) = dims
    cat = c0 + gr
    (ig_hbm, pool_hbm, stats, sum_a, sum_c) = rest[:5]
    rest = list(rest[5:])

    def take(n):
        taken = rest[:n]
        del rest[:n]
        return taken

    (xv, av, sv, mv, pmv, px, tin, ting, ev, eg, cotv) = take(11)
    (bnv, a2v, s2v, gv, ggv, gmv) = take(6)
    (wlf, wlb, wlg, wff, wfb, wfn, wgf, wft, wfm, wbm, pmat, umat, cvec, poolv, gt) = take(15)
    (x_sems, io_sems, cot_sems, halo_sems, gg_sems, pool_sems) = take(6)
    small = [take(4) for _ in range(4)]
    small.append(small[0][:2] + take(2))
    small.append(take(4))
    big = [take(7) for _ in range(2)]
    up = take(1)[0]
    local_b = local_c = big[1][0]

    r, b = lax.axis_index("rows"), lax.axis_index("batch")
    place, counts = (r, b), (rows, batch)
    n_pix, n_cell = images * 64, images * 16
    tiles = images // TILE_IMGS
    tp, tc = TILE_IMGS * 64, TILE_IMGS * 16

    w_copies = [
        pltpu.make_async_copy(wf_hbm, wff, io_sems.at[0]),
        pltpu.make_async_copy(wg_hbm, wgf, io_sems.at[1]),
        pltpu.make_async_copy(wl_hbm, wlf, io_sems.at[2]),
    ]
    w_copies[1].start()
    x_copies = [
        pltpu.make_async_copy(x_hbm.at[pl.ds(pl.multiple_of(t * tp, tp), tp)], xv.at[pl.ds(pl.multiple_of(t * tp, tp), tp)], x_sems.at[t]) for t in range(tiles)
    ]
    for copy in x_copies:
        copy.start()
    w_copies[0].start()
    w_copies[2].start()
    cot_own = pltpu.make_async_copy(
        cot_hbm.at[:, pl.ds(pl.multiple_of(r * 16, 16), 16)], cotv.at[pl.ds(r * own, own)], io_sems.at[3]
    )
    cot_own.start()
    barrier = pltpu.get_barrier_semaphore()
    for axis, me, count in (("rows", r, rows), ("batch", b, batch)):
        for step in range(1, count):
            pl.semaphore_signal(barrier, inc=1, device_id={axis: lax.rem(me + step, count)}, device_id_type=MESH)

    a_id = lax.broadcasted_iota(jnp.int32, (tc, tp), 0)
    b_id = lax.broadcasted_iota(jnp.int32, (tc, tp), 1)
    hit = (a_id // 8 == b_id // 32) & (a_id % 8 == (b_id % 16) // 2)
    pmat[...] = jnp.where(hit, 1.0, 0.0).astype(BF16)
    a_id = lax.broadcasted_iota(jnp.int32, (tp, tc), 1)
    b_id = lax.broadcasted_iota(jnp.int32, (tp, tc), 0)
    hit = (a_id // 8 == b_id // 32) & (a_id % 8 == (b_id % 16) // 2)
    umat[...] = jnp.where(hit, 1.0, 0.0).astype(BF16)

    pix = lax.broadcasted_iota(jnp.int32, (64, 1), 0)
    inside = jnp.where((r * 4 + pix // 16 < SMALL) & (pix % 16 < SMALL), 1.0, 0.0)
    cell = lax.broadcasted_iota(jnp.int32, (16, 1), 0)
    inside_cell = jnp.where((r * 4 + cell // 8 * 2 < SMALL) & (cell % 8 * 2 < SMALL), 1.0, 0.0)
    inside_above = jnp.where((r * 4 - 1 < SMALL) & (cell < SMALL), 1.0, 0.0)
    inside_below = jnp.where((r * 4 + 4 < SMALL) & (cell < SMALL), 1.0, 0.0)
    have_above = jnp.where(r > 0, 1.0, 0.0)
    have_below = jnp.where(r < rows - 1, 1.0, 0.0)
    inside_count = jnp.clip(SMALL - r * 4, 0, 4) * SMALL

    copy_id = lax.broadcasted_iota(jnp.int32, (LANES, gr), 0)
    lane_id = lax.broadcasted_iota(jnp.int32, (LANES, gr), 1)
    spread = jnp.where((copy_id % gr == lane_id) & (copy_id < 3 * gr), 1.0, 0.0).astype(BF16)
    w_copies[1].wait()
    wgb = wgf[...].astype(BF16)
    gap = lax.broadcasted_iota(jnp.int32, (9 * bot, bot), 0) - 9 * lax.broadcasted_iota(jnp.int32, (9 * bot, bot), 1)
    wft[...] = jnp.zeros_like(wft)
    for dh in range(3):
        for dw in range(3):
            pick = jnp.where(gap == 3 * dh + dw, 1.0, 0.0).astype(BF16)
            tap = dot(wgb, pick, 1, 0)
            for c in range(3):
                wft[dh, LANES * dw + gr * c : LANES * dw + gr * (c + 1), :] = tap
            wft[3, LANES * dw + gr * dh : LANES * dw + gr * (dh + 1), :] = tap
    for dh in range(3):
        wfm[dh] = wft[dh].T.astype(BF16)
    wbm[...] = wft[3].astype(BF16)


    tiles_c0, blocks_c0 = lane_tiles(c0), lane_blocks(c0)

    def sums_body(t, carry):
        acc, acc2, count = carry
        pltpu.make_async_copy(x_hbm.at[pl.ds(pl.multiple_of(t * tp, tp), tp)], xv.at[pl.ds(pl.multiple_of(t * tp, tp), tp)], x_sems.at[t]).wait()
        for q in range(TILE_IMGS):
            img = t * TILE_IMGS + q
            is_small = flags[img] > 0
            count = count + jnp.where(is_small, inside_count, 64)
            mask = jnp.where(is_small, inside, 1.0)
            mv[pl.ds(img * 64, 64), :] = jnp.broadcast_to(mask, (64, LANES))
            pmv[pl.ds(img * 16, 16), :] = jnp.broadcast_to(jnp.where(is_small, inside_cell, 1.0), (16, LANES))
        squares, firsts = [], []
        for k, (j, w) in enumerate(tiles_c0):
            total = acc2[k]
            for i in range(0, tp, 32):
                x = xv[pl.ds(pl.multiple_of(t * tp + i, 32), 32), j : j + w].astype(F32)
                total = total + fold_rows(x * x * mv[pl.ds(pl.multiple_of(t * tp + i, 32), 32), 0:w])
            squares.append(total)
        for k, (j, w) in enumerate(blocks_c0):
            cells = dot(pmat[...], xv[pl.ds(pl.multiple_of(t * tp, tp), tp), j : j + w], 1, 0) * pmv[pl.ds(pl.multiple_of(t * tc, tc), tc), 0:1]
            px[pl.ds(pl.multiple_of(t * tc, tc), tc), j : j + w] = cells
            firsts.append(acc[k] + fold_rows(cells))
        return tuple(firsts), tuple(squares), count

    acc, acc2, count = lax.fori_loop(0, tiles, sums_body, (zeros_for(blocks_c0), zeros_for(tiles_c0), jnp.int32(0)))
    acc, acc2 = jnp.concatenate(acc, axis=1), jnp.concatenate(acc2, axis=1)
    red1 = VectorReduce(place, counts, small[0])
    slot = small[0][0]
    span = len(tiles_c0)
    pack_row(slot, r, 0, row_sum(acc))
    pack_row(slot, r, span, row_sum(acc2))
    slot[r, 2 * span : 2 * span + 1, :] = jnp.full((1, LANES), count.astype(F32))
    pl.semaphore_wait(barrier, rows - 1 + batch - 1)
    red1.start()

    w_copies[0].wait()
    w_copies[2].wait()
    wfb[...] = wff[...].astype(BF16)
    wfn[...] = wff[...].T.astype(BF16)
    wlb[...] = wlf[...].astype(BF16)
    red1.middle()
    cot_copies = []
    for step in range(1, rows):
        peer = lax.rem(r + step, rows)
        cot_copies.append(
            pltpu.make_async_remote_copy(
                src_ref=cot_hbm.at[:, pl.ds(pl.multiple_of(peer * 16, 16), 16)],
                dst_ref=cotv.at[pl.ds(r * own, own)],
                send_sem=cot_sems.at[0, step],
                recv_sem=cot_sems.at[1, step],
                device_id={"rows": peer},
                device_id_type=MESH,
            )
        )
    for copy in cot_copies:
        copy.start()

    wlg[...] = dot(spread, wlf[c0:cat, :].astype(BF16), 1, 0).astype(BF16)
    total = red1.finish()
    count_all = total[2 * span : 2 * span + 1, 0:1]
    per = 1.0 / count_all
    mean1 = unpack_row(total, 0, c0) * per
    inv1 = lax.rsqrt(unpack_row(total, span, c0) * per - mean1 * mean1 + EPSILON)
    gain1, shift1 = params[0:1, 0:c0], params[1:2, 0:c0]
    gain2, shift2 = params[0:1, c0 : c0 + bot], params[1:2, c0 : c0 + bot]
    gain3, shift3 = params[0:1, c0 + bot : 2 * c0 + bot], params[1:2, c0 + bot : 2 * c0 + bot]
    gaing, shiftg = params[0:1, 2 * c0 + bot :], params[1:2, 2 * c0 + bot :]
    half_a = 0.5 * gain1 * inv1
    half_b = 0.5 * shift1 - mean1 * half_a
    trans_a = gain3 * inv1
    trans_b = shift3 - mean1 * trans_a
    cvec[0:1, 0:c0] = half_a
    cvec[1:2, 0:c0] = half_b
    cvec[2:3, 0:c0] = 0.25 * trans_a
    cvec[3:4, 0:c0] = trans_b
    cvec[4:5, 0:c0] = mean1
    cvec[5:6, 0:c0] = inv1
    cvec[6:7, 0:c0] = gain1 * inv1
    cvec[7:8, 0:c0] = trans_a

    def first_act(t):
        for j, w in tiles_c0:
            cols = slice(j, j + w)
            scale, shift = cvec[0:1, cols], cvec[1:2, cols]
            for i in range(0, tp, 32):
                at = pl.ds(pl.multiple_of(t * tp + i, 32), 32)
                h = xv[at, cols].astype(F32) * scale + shift
                th = jnp.tanh(h)
                ht = h * th
                av[at, cols] = (h + ht).astype(BF16)
                sv[at, cols] = ((1.0 + th) * (1.0 + (h - ht))).astype(BF16)
            scale, shift = cvec[2:3, cols], cvec[3:4, cols]
            for i in range(0, tc, 32):
                ct = pl.ds(pl.multiple_of(t * tc + i, 32), 32)
                tin[ct, cols] = (px[ct, cols] * scale + pmv[ct, 0:w] * shift).astype(BF16)

    def first_product(t, carry):
        acc, acc2 = carry
        at = pl.ds(pl.multiple_of(t * tp, tp), tp)
        value = dot(av[at, :], wfn[...], 1, 0) * mv[at, 0:1]
        bnv[pl.ds(t * TILE_IMGS, TILE_IMGS)] = value.reshape(TILE_IMGS, 4, 16, bot)
        return acc + fold_rows(value), acc2 + fold_rows(value * value)

    def first_body(t, carry):
        carry = first_product(t - 1, carry)
        first_act(t)
        return carry

    zero = jnp.zeros((8, bot), F32)
    first_act(0)
    acc, acc2 = first_product(tiles - 1, lax.fori_loop(1, tiles, first_body, (zero, zero)))
    red2 = VectorReduce(place, counts, small[1])
    slot = small[1][0]
    pack_row(slot, r, 0, row_sum(acc))
    pack_row(slot, r, 2, row_sum(acc2))
    red2.start()
    a2v[:, 1] = bnv[:, 0].astype(BF16)
    a2v[:, 4] = bnv[:, 3].astype(BF16)

    def edge_copy(ref, sems, side, send):
        return pltpu.make_async_remote_copy(
            src_ref=ref.at[:, 1 + 3 * side],
            dst_ref=ref.at[:, 5 - 5 * side if send else 5 * side],
            send_sem=sems.at[0, side],
            recv_sem=sems.at[1, 1 - side if send else side],
            device_id={"rows": lax.rem(r + rows - 1 + 2 * side, rows)},
            device_id_type=MESH,
        )

    def on_edges(action):
        pl.when(r > 0)(lambda: action(0))
        pl.when(r < rows - 1)(lambda: action(1))

    on_edges(lambda side: edge_copy(a2v, halo_sems, side, True).start())
    cot_own.wait()
    for copy in cot_copies:
        copy.wait()
    red2.middle()

    cot_all = cotv[...].reshape(n_cell, trans)
    eg[...] = dot(cot_all, wlg[...], 1, 1)
    acc_e, acc_ex = [], []
    for j, w in blocks_c0:
        value = dot(cot_all, wlb[j : j + w, :], 1, 1)
        ev[:, j : j + w] = value
        total, total2 = jnp.zeros((8, w), F32), jnp.zeros((8, w), F32)
        for i in range(0, n_cell, 32):
            piece = value[i : i + 32]
            total = total + fold_rows(piece * pmv[i : i + 32, 0:1])
            total2 = total2 + fold_rows(piece * px[i : i + 32, j : j + w])
        acc_e.append(total)
        acc_ex.append(total2)
    acc_e, acc_ex = jnp.concatenate(acc_e, axis=1), jnp.concatenate(acc_ex, axis=1)
    red6 = VectorReduce(place, counts, small[5])
    pack_row(small[5][0], r, 0, row_sum(acc_e))
    pack_row(small[5][0], r, span, row_sum(acc_ex))
    red_a = BlockReduce(place, counts, big[0])
    local_a = big[0][0]
    stride_a = round_up(c0, 16)
    step_rows = 512
    for i in range(0, c0, step_rows):
        n = min(step_rows, c0 - i)
        value = dot(tin[:, i : i + n], cot_all, 0, 0)
        for j in range(0, trans, LANES):
            w = min(LANES, trans - j)
            local_a[j // LANES * stride_a + i : j // LANES * stride_a + i + n, 0:w] = value[:, j : j + w]

    total = red2.finish()
    mean2 = unpack_row(total, 0, bot) * per
    inv2 = lax.rsqrt(unpack_row(total, 2, bot) * per - mean2 * mean2 + EPSILON)
    half_a2 = 0.5 * gain2 * inv2
    half_b2 = 0.5 * shift2 - mean2 * half_a2
    red6.start()
    red_a.start()

    on_edges(lambda side: edge_copy(a2v, halo_sems, side, True).wait_send())

    def middle_body(t, carry):
        imgs = pl.ds(t * TILE_IMGS, TILE_IMGS)
        at = pl.ds(pl.multiple_of(t * tp, tp), tp)
        h = bnv[imgs].reshape(tp, bot) * half_a2 + half_b2
        th = jnp.tanh(h)
        ht = h * th
        mask = mv[at, 0:1]
        a2v[imgs, 1:5] = ((h + ht) * mask).astype(BF16).reshape(TILE_IMGS, 4, 16, bot)
        s2v[at, :] = ((1.0 + th) * (1.0 + (h - ht)) * (0.5 * mask)).astype(BF16)
        return carry

    lax.fori_loop(0, tiles, middle_body, 0)

    on_edges(lambda side: edge_copy(a2v, halo_sems, side, False).wait_recv())
    for side, row, fits, have in ((0, 0, inside_above, have_above), (1, 5, inside_below, have_below)):

        def edge_body(t, carry, side=side, row=row, fits=fits, have=have):
            size = 16
            imgs = pl.ds(pl.multiple_of(t * size, size), size)
            h = a2v[imgs, row].astype(F32).reshape(size * 16, bot) * half_a2 + half_b2
            value = h + h * jnp.tanh(h)
            mask = [jnp.where(flags[t * size + q] > 0, fits, 1.0) * have for q in range(size)]
            value = jnp.where(jnp.concatenate(mask, axis=0) > 0.0, value, 0.0)
            a2v[imgs, row] = value.astype(BF16).reshape(size, 16, bot)
            return carry

        lax.fori_loop(0, images // 16, edge_body, 0)
    red_a.step_b()
    red6.middle()

    col = lax.broadcasted_iota(jnp.int32, (tp, 1), 0) % 16
    not_first, not_last = jnp.where(col > 0, 1.0, 0.0), jnp.where(col < 15, 1.0, 0.0)

    def growth_body(t, carry):
        acc, acc2, acc_e, acc_eg = carry
        imgs = pl.ds(t * TILE_IMGS, TILE_IMGS)
        at, ct = pl.ds(pl.multiple_of(t * tp, tp), tp), pl.ds(pl.multiple_of(t * tc, tc), tc)
        z = dot(a2v[imgs, 0:4].reshape(tp, bot), wfm[0], 1, 0)
        z = z + dot(a2v[imgs, 1:5].reshape(tp, bot), wfm[1], 1, 0)
        z = z + dot(a2v[imgs, 2:6].reshape(tp, bot), wfm[2], 1, 0)
        left = pltpu.roll(z[:, 0:LANES], 1, 0) * not_first
        right = pltpu.roll(z[:, 2 * LANES :], tp - 1, 0) * not_last
        g = left + z[:, LANES : 2 * LANES] + right
        gv[at, :] = g
        gm = g * mv[at, :]
        high, low = split(gm)
        pg = dot(pmat[...], high, 1, 0) + dot(pmat[...], low, 1, 0)
        gt[ct, :] = pg
        e = eg[ct, :]
        return acc + fold_rows(pg), acc2 + fold_rows(gm * g), acc_e + fold_rows(e * pmv[ct, :]), acc_eg + fold_rows(e * pg)

    zero = jnp.zeros((8, LANES), F32)
    sums = lax.fori_loop(0, tiles, growth_body, (zero,) * 4)
    red3 = VectorReduce(place, counts, small[2])
    slot = small[2][0]
    for j in range(4):
        slot[r, j : j + 1, :] = row_sum(sums[j])
    red3.start()

    px[:, 0:trans] = dot(tin[...], wlb[0:c0, :], 1, 0)
    red3.middle()
    red_a.step_c()
    poolv[...] = jnp.zeros_like(poolv)
    for c in range(3):
        poolv[0:1, gr * c : gr * (c + 1)] = gaing
        poolv[1:2, gr * c : gr * (c + 1)] = shiftg
    gain_g, shift_g = poolv[0:1, :], poolv[1:2, :]
    total = red3.finish()
    mean_g = total[0:1, :] * per
    inv_g = lax.rsqrt(total[1:2, :] * per - mean_g * mean_g + EPSILON)
    shift_grad_g = total[2:3, :]
    gain_grad_g = inv_g * (0.25 * total[3:4, :] - mean_g * shift_grad_g)
    scale_g = gain_g * inv_g
    slope_g = scale_g * gain_grad_g * inv_g * per
    const_g = slope_g * mean_g - scale_g * shift_grad_g * per
    off_g = shift_g - mean_g * scale_g

    def grad_body(t, carry):
        imgs = pl.ds(t * TILE_IMGS, TILE_IMGS)
        at, ct = pl.ds(pl.multiple_of(t * tp, tp), tp), pl.ds(pl.multiple_of(t * tc, tc), tc)
        high, low = split(eg[ct, :] * (0.25 * scale_g) + const_g)
        wide = dot(umat[...], high, 1, 0) + dot(umat[...], low, 1, 0)
        gg = (wide - gv[at, :] * slope_g) * mv[at, :]
        ggv[imgs, 1:5] = gg.astype(BF16).reshape(TILE_IMGS, 4, 16, LANES)
        ting[ct, :] = (gt[ct, :] * (0.25 * scale_g) + pmv[ct, :] * off_g).astype(BF16)
        return carry

    lax.fori_loop(0, tiles, grad_body, 0)

    on_edges(lambda side: edge_copy(ggv, gg_sems, side, True).start())

    @pl.when(r == 0)
    def _():
        ggv[:, 0] = jnp.zeros((images, 16, LANES), BF16)

    @pl.when(r == rows - 1)
    def _():
        ggv[:, 5] = jnp.zeros((images, 16, LANES), BF16)

    lane = lax.broadcasted_iota(jnp.int32, (1, LANES), 1)

    def pool_body(t, carry):
        ct = pl.ds(pl.multiple_of(t * 256, 256), 256)
        own_g = jnp.where(lane < gr, ting[ct, :].astype(F32), 0.0).astype(BF16)
        value = px[ct, 0:trans] + dot(own_g, wlg[...], 1, 0)
        hpool[pl.ds(t * 16, 16)] = value.astype(BF16).reshape(16, 16, trans)
        return carry

    hpool = take(1)[0]
    lax.fori_loop(0, n_cell // 256, pool_body, 0)
    pool_copies = []
    for step in range(1, rows):
        peer = lax.rem(r + step, rows)
        pool_copies.append(
            pltpu.make_async_remote_copy(
                src_ref=hpool.at[pl.ds(peer * own, own)],
                dst_ref=pool_hbm.at[:, pl.ds(pl.multiple_of(r * 16, 16), 16)],
                send_sem=pool_sems.at[0, step],
                recv_sem=pool_sems.at[1, step],
                device_id={"rows": peer},
                device_id_type=MESH,
            )
        )
    red_a.step_d()
    red_c = BlockReduce(place, counts, big[1])
    local_c[...] = jnp.zeros_like(local_c)
    base_c = len(tiles_c0) * round_up(bot, 8)
    stride_g = round_up(gr, 8)
    value = dot(ting[...], cot_all, 0, 0)
    for j in range(0, trans, LANES):
        w = min(LANES, trans - j)
        top = base_c + j // LANES * stride_g
        local_c[top : top + gr, 0:w] = value[0:gr, j : j + w]
    base_taps = base_c + -(-trans // LANES) * stride_g

    on_edges(lambda side: edge_copy(ggv, gg_sems, side, True).wait_send())
    on_edges(lambda side: edge_copy(ggv, gg_sems, side, False).wait_recv())
    lanes_all = lax.broadcasted_iota(jnp.int32, (tp, LANES), 1)
    wft[0] = jnp.zeros(wft.shape[1:], F32)

    def conv_body(t, carry):
        acc, acc2 = carry
        imgs = pl.ds(t * TILE_IMGS, TILE_IMGS)
        at = pl.ds(pl.multiple_of(t * tp, tp), tp)
        above = ggv[imgs, 0:4].reshape(tp, LANES).astype(F32)
        here = ggv[imgs, 1:5].reshape(tp, LANES).astype(F32)
        below = ggv[imgs, 2:6].reshape(tp, LANES).astype(F32)
        mixed = jnp.where(lanes_all < gr, below, jnp.where(lanes_all < 2 * gr, here, jnp.where(lanes_all < 3 * gr, above, 0.0)))
        from_right = pltpu.roll(mixed, tp - 1, 0) * not_last
        from_left = pltpu.roll(mixed, 1, 0) * not_first
        patch = jnp.concatenate([from_right, mixed, from_left], axis=1).astype(BF16)
        gm = dot(patch, wbm[...], 1, 0) * s2v[at, :].astype(F32)
        gmv[at, :] = gm
        wft[0] += dot(patch, a2v[imgs, 1:5].reshape(tp, bot), 0, 0)
        hat = bnv[imgs].reshape(tp, bot) - mean2
        return acc + fold_rows(gm), acc2 + fold_rows(gm * hat)

    zero = jnp.zeros((8, bot), F32)
    acc, acc2 = lax.fori_loop(0, tiles, conv_body, (zero, zero))
    red4 = VectorReduce(place, counts, small[3])
    slot = small[3][0]
    pack_row(slot, r, 0, row_sum(acc))
    pack_row(slot, r, 2, row_sum(acc2))
    red4.start()
    red4.middle()
    red_a.step_e()
    gap = lax.broadcasted_iota(jnp.int32, (bot, 9 * bot), 1) - 9 * lax.broadcasted_iota(jnp.int32, (bot, 9 * bot), 0)
    value = jnp.zeros((gr, 9 * bot), F32)
    for dh in range(3):
        for dw in range(3):
            pick = jnp.where(gap == 3 * dh + dw, 1.0, 0.0).astype(BF16)
            tap = wft[0, LANES * dw + gr * dh : LANES * dw + gr * (dh + 1), :]
            high, low = split(tap)
            value = value + (dot(high, pick, 1, 0) + dot(low, pick, 1, 0))
    for j in range(0, 9 * bot, LANES):
        w = min(LANES, 9 * bot - j)
        top = base_taps + j // LANES * stride_g
        local_c[top : top + gr, 0:w] = value[:, j : j + w]
    total = red4.finish()
    shift_grad2 = unpack_row(total, 0, bot)
    gain_grad2 = inv2 * unpack_row(total, 2, bot)
    scale2 = gain2 * inv2
    slope2 = scale2 * gain_grad2 * inv2 * per
    const2 = scale2 * shift_grad2 * per - slope2 * mean2
    for copy in pool_copies:
        copy.start()
    pool_own = pltpu.make_async_copy(
        hpool.at[pl.ds(r * own, own)], pool_hbm.at[:, pl.ds(pl.multiple_of(r * 16, 16), 16)], io_sems.at[4]
    )
    pool_own.start()

    stride_f = round_up(bot, 8)
    blocks = -(-c0 // LANES)

    def bottleneck_body(t, carry):
        imgs = pl.ds(t * TILE_IMGS, TILE_IMGS)
        at = pl.ds(pl.multiple_of(t * tp, tp), tp)
        bn = bnv[imgs].reshape(tp, bot)
        gb = ((gmv[at, :] * scale2 - bn * slope2 - const2) * mv[at, 0:1]).astype(BF16)
        s2v[at, :] = gb
        grad = dot(gb, av[at, :], 0, 0)
        for k, (j, w) in enumerate(tiles_c0):
            local_b[k * stride_f : k * stride_f + bot, 0:w] += grad[:, j : j + w]
        return carry

    lax.fori_loop(0, tiles, bottleneck_body, 0)
    red_c.start()

    def back_body(t, carry):
        acc, acc2 = carry
        at = pl.ds(pl.multiple_of(t * tp, tp), tp)
        gb = s2v[at, :]
        sums, cross = [], []
        for k, (j, w) in enumerate(blocks_c0):
            cols = slice(j, j + w)
            value = dot(gb, wfb[:, cols], 1, 0)
            total, total2 = acc[k], acc2[k]
            for i in range(0, tp, 32):
                part = pl.ds(pl.multiple_of(t * tp + i, 32), 32)
                gf = value[i : i + 32] * sv[part, cols].astype(F32)
                av[part, cols] = gf.astype(BF16)
                total = total + fold_rows(gf)
                total2 = total2 + fold_rows(gf * xv[part, cols].astype(F32))
            sums.append(total)
            cross.append(total2)
        return tuple(sums), tuple(cross)

    zero = zeros_for(blocks_c0)
    sums = lax.fori_loop(0, tiles // 2, back_body, (zero, zero))
    red_c.step_b()
    sums = lax.fori_loop(tiles // 2, tiles, back_body, sums)
    acc, acc2 = jnp.concatenate(sums[0], axis=1), jnp.concatenate(sums[1], axis=1)
    red5 = VectorReduce(place, counts, small[4])
    pack_row(small[4][0], r, 0, row_sum(acc))
    pack_row(small[4][0], r, span, row_sum(acc2))
    red5.start()
    red_c.step_c()
    cvec[0:1, 0:c0] = 0.25 * cvec[7:8, 0:c0]
    cvec[2:3, 0:c0] = 0.5 * cvec[6:7, 0:c0]

    def part_grad(t, carry):
        for q in range(TILE_IMGS):
            img = t * TILE_IMGS + q
            for j, w in tiles_c0:
                cols, full = slice(j, j + w), slice(j, j + LANES)
                ct = pl.ds(pl.multiple_of(img * 16, 16), 16)
                cells = ev[ct, full] * cvec[0:1, full] * pmv[ct, :]
                up[j // LANES, pl.ds(0, 16, stride=2), :] = cells
                up[j // LANES, pl.ds(1, 16, stride=2), :] = cells
                scale = cvec[2:3, cols]
                for half in range(2):
                    at = pl.ds(pl.multiple_of(img * 64 + half * 32, 32), 32)
                    wide_cells = up[j // LANES, half * 16 : half * 16 + 16, 0:w]
                    wide_cells = jnp.concatenate([wide_cells, wide_cells], axis=0)
                    sv[at, cols] = (wide_cells + av[at, cols].astype(F32) * scale).astype(BF16)
        return carry

    lax.fori_loop(0, tiles // 4, part_grad, 0)
    red5.middle()
    lax.fori_loop(tiles // 4, 7 * tiles // 12, part_grad, 0)
    red_c.step_d()
    lax.fori_loop(7 * tiles // 12, tiles, part_grad, 0)
    red_a.step_f()
    total = red5.finish()
    red_c.step_e()
    mean1, inv1 = cvec[4:5, 0:c0], cvec[5:6, 0:c0]
    scale1, scale3 = cvec[6:7, 0:c0], cvec[7:8, 0:c0]
    shift_grad1 = 0.5 * unpack_row(total, 0, c0)
    gain_grad1 = inv1 * (0.5 * unpack_row(total, span, c0) - mean1 * shift_grad1)
    total = red6.finish()
    shift_grad3 = unpack_row(total, 0, c0)
    gain_grad3 = inv1 * (0.25 * unpack_row(total, span, c0) - mean1 * shift_grad3)
    slope1 = (scale3 * gain_grad3 + scale1 * gain_grad1) * inv1 * per
    const1 = (scale3 * shift_grad3 + scale1 * shift_grad1) * per - slope1 * mean1
    stats[...] = jnp.zeros_like(stats)
    stats[0:1, 0:c0] = gain_grad1
    stats[1:2, 0:c0] = shift_grad1
    stats[2:3, 0:bot] = gain_grad2
    stats[3:4, 0:bot] = shift_grad2
    stats[4:5, 0:c0] = gain_grad3
    stats[5:6, 0:c0] = shift_grad3
    stats[6:7, 0:LANES] = gain_grad_g
    stats[7:8, 0:LANES] = shift_grad_g
    stats[8:9, :] = jnp.broadcast_to(count_all, (1, stats.shape[1]))
    cvec[1:2, 0:c0] = const1
    cvec[3:4, 0:c0] = slope1

    def out_copy(t):
        at = pl.ds(pl.multiple_of(t * tp, tp), tp)
        return pltpu.make_async_copy(av.at[at], ig_hbm.at[at], x_sems.at[t])

    def last_body(t, carry):
        for q in range(TILE_IMGS):
            img = t * TILE_IMGS + q
            for j, w in tiles_c0:
                cols = slice(j, j + w)
                slope, const = cvec[3:4, cols], cvec[1:2, cols]
                for i in range(0, 64, 32):
                    at = pl.ds(pl.multiple_of(img * 64 + i, 32), 32)
                    value = (xv[at, cols].astype(F32) * slope + const) * mv[at, 0:w]
                    av[at, cols] = (sv[at, cols].astype(F32) - value).astype(BF16)
        out_copy(t).start()
        return carry

    lax.fori_loop(0, tiles // 2, last_body, 0)
    red_c.step_f()
    lax.fori_loop(tiles // 2, tiles, last_body, 0)
    red_a.finish()
    out_a = pltpu.make_async_copy(big[0][5], sum_a, io_sems.at[0])
    out_a.start()
    red_c.finish()
    out_c = pltpu.make_async_copy(big[1][5], sum_c, io_sems.at[2])
    out_c.start()
    pool_own.wait()
    for copy in pool_copies:
        copy.wait()
    for t in range(tiles):
        out_copy(t).wait()
    out_a.wait()
    out_c.wait()


def mm3(a, b, ca, cb):
    left = jnp.concatenate([a[0], a[0], a[1]], axis=ca)
    right = jnp.concatenate([b[0], b[1], b[0]], axis=cb)
    return dot(left, right, ca, cb)


def orthogonal_steps(pads, sides, sizes, found):
    start, gram, prod, ones = [], [], [], []
    for pad, side, size in zip(pads, sides, sizes):
        halves = unit_norm(pad)
        start.append(halves)
        gram.append(mm3(halves, halves, side, side))
        full = gram[-1].shape[0]
        i, j = (lax.broadcasted_iota(jnp.int32, (full, full), d) for d in (0, 1))
        ones.append((i == j) & (i < size))
        prod.append(None)
    yield
    for k in range(NS_STEPS):
        halves = [split(g) for g in gram]
        square = [mm3(h, h, 1, 0) for h in halves]
        poly = [jnp.where(o, QUINTIC_A, 0.0) + QUINTIC_B * g + QUINTIC_C * s for o, g, s in zip(ones, gram, square)]
        poly_h = [split(p) for p in poly]
        if k < NS_STEPS - 1:
            mid = [split(mm3(h, p, 1, 0)) for h, p in zip(halves, poly_h)]
            gram = [mm3(m, p, 1, 0) for m, p in zip(mid, poly_h)]
        prod = [p if k == 0 else split(mm3(q, p, 1, 0)) for q, p in zip(prod, poly_h)]
        if k == NS_STEPS - 1:
            found.extend(zip(start, prod))
        yield


def unit_norm(pad):
    value = pad[...]
    norm = jnp.sqrt(jnp.sum(jnp.sum(value * value, axis=0, keepdims=True), axis=1, keepdims=True)) + TINY
    pad[...] = value / norm
    return split(pad[...])


class LoopedOrthogonal:
    def __init__(self, valid, refs):
        self.valid = valid
        self.stack, self.poly, self.mid = refs
        self.full = self.poly.shape[1]

    @staticmethod
    def scratch(full):
        return [pltpu.VMEM((2, 2 * full, full), BF16), pltpu.VMEM((2, full, full), BF16), pltpu.VMEM((2, full, full), BF16)]

    def store(self, ref, start, value):
        high, low = split(value)
        ref[0, start : start + value.shape[0]] = high
        ref[1, start : start + value.shape[0]] = low

    def unit(self, scale):
        i, j = (lax.broadcasted_iota(jnp.int32, (self.full, self.full), d) for d in (0, 1))
        return jnp.where((i == j) & self.valid(i), scale, 0.0)

    def begin(self, gram):
        self.store(self.stack, 0, gram)
        self.stack[0, self.full :] = self.unit(1.0).astype(BF16)
        self.stack[1, self.full :] = jnp.zeros((self.full, self.full), BF16)

    def polynomial(self):
        n = self.full
        high, low = self.stack[0, 0:n], self.stack[1, 0:n]
        square = mm3((high, low), (high, low), 1, 0)
        gram = high.astype(F32) + low.astype(F32)
        self.store(self.poly, 0, self.unit(QUINTIC_A) + QUINTIC_B * gram + QUINTIC_C * square)

    def step(self, k, carry):
        n = self.full
        self.polynomial()
        poly = (self.poly[0], self.poly[1])
        both = mm3((self.stack[0], self.stack[1]), poly, 1, 0)
        self.store(self.mid, 0, both[0:n])
        self.store(self.stack, n, both[n:])
        self.store(self.stack, 0, mm3((self.mid[0], self.mid[1]), poly, 1, 0))
        return carry

    def light_step(self, k, carry):
        n = self.full
        high = self.stack[0, 0:n]
        gram = high.astype(F32) + self.stack[1, 0:n].astype(F32)
        poly = (QUINTIC_B * gram + QUINTIC_C * dot(high, high, 1, 0)).astype(BF16)
        self.poly[0] = poly
        both = self.stack[0].astype(F32) + self.stack[1].astype(F32)
        both = QUINTIC_A * both + dot(self.stack[0], poly, 1, 0)
        self.store(self.stack, n, both[n:])
        mid = both[0:n]
        self.store(self.stack, 0, QUINTIC_A * mid + dot(mid.astype(BF16), self.poly[0], 1, 0))
        return carry

    def finish(self):
        n = self.full
        self.polynomial()
        return split(mm3((self.stack[0, n:], self.stack[1, n:]), (self.poly[0], self.poly[1]), 1, 0))


def sum_rows(ref, top, count, width):
    base = top // 16 * 16
    size = min(round_up(top - base + count, 16), ref.shape[0] - base)
    return ref[base : base + size, :].astype(F32)[top - base : top - base + count, 0:width]


def transition_moment(c0, gr, trans, ml, sum_a, sum_c, base, put):
    stride_a, stride_g = round_up(c0, 16), round_up(gr, 8)
    for j, w in lane_tiles(trans):
        k = j // LANES
        put(slice(0, c0), slice(j, j + w), MOMENTUM_DECAY * ml[0:c0, j : j + w] + sum_rows(sum_a, k * stride_a, c0, w))
        rows = slice(c0, c0 + gr)
        put(rows, slice(j, j + w), MOMENTUM_DECAY * ml[rows, j : j + w] + sum_rows(sum_c, base + k * stride_g, gr, w))


def update_kernel(dims, ig_in, pool_in, wl_hbm, ml_hbm, stats, sum_a, sum_c, params, p_moment, wf, wg, mf, mg, *refs):
    (c0, bot, gr, trans) = dims
    cat = c0 + gr
    (ig_out, pool_out, wl_out, ml_out, p_moment_new, params_new, mf_new, mg_new, wf_new, wg_new) = refs[:10]
    (lpad, spad, igv, poolv, wl, ml, sems) = refs[10:17]
    low = round_up(bot, 8)
    loops = [
        LoopedOrthogonal(lambda i: i < trans, refs[17:20]),
        LoopedOrthogonal(lambda i: (i < bot) | ((i >= low) & (i < low + gr)), refs[20:23]),
    ]
    loads = [pltpu.make_async_copy(ml_hbm, ml, sems.at[0, 0]), pltpu.make_async_copy(wl_hbm, wl, sems.at[0, 1])]
    loads += [pltpu.make_async_copy(ig_in, igv, sems.at[0, 2]), pltpu.make_async_copy(pool_in, poolv, sems.at[0, 3])]
    stores = [pltpu.make_async_copy(ml, ml_out, sems.at[1, 0]), pltpu.make_async_copy(wl, wl_out, sems.at[1, 1])]
    stores += [pltpu.make_async_copy(igv, ig_out, sems.at[1, 2]), pltpu.make_async_copy(poolv, pool_out, sems.at[1, 3])]
    for copy in loads:
        copy.start()

    count = stats[8:9, 0:1]
    step = NORM_RATE * lax.rsqrt(count)
    spans = ((0, c0, 0), (c0, bot, 2), (c0 + bot, c0, 4), (2 * c0 + bot, gr, 6))
    for start, width, row in spans:
        moment = MOMENTUM_DECAY * p_moment[:, start : start + width] + stats[row : row + 2, 0:width]
        p_moment_new[:, start : start + width] = moment
        params_new[:, start : start + width] = params[:, start : start + width] - step * moment

    stride_g, stride_f = round_up(gr, 8), round_up(bot, 8)
    lpad[...] = jnp.zeros_like(lpad)
    spad[...] = jnp.zeros_like(spad)
    base = len(lane_tiles(c0)) * stride_f
    for j, w in lane_tiles(c0):
        new = MOMENTUM_DECAY * mf[:, j : j + w] + sum_rows(sum_c, j // LANES * stride_f, bot, w)
        mf_new[:, j : j + w] = new
        spad[0:bot, j : j + w] = new
    loads[0].wait()

    def put(at, cols, value):
        ml[at, cols] = value
        lpad[at, cols] = value

    transition_moment(c0, gr, trans, ml, sum_a, sum_c, base, put)
    stores[0].start()
    base = base + len(lane_tiles(trans)) * stride_g
    for j, w in lane_tiles(9 * bot):
        new = MOMENTUM_DECAY * mg[:, j : j + w] + sum_rows(sum_c, base + j // LANES * stride_g, gr, w)
        mg_new[:, j : j + w] = new
        spad[low : low + gr, j : j + w] = new
    halves = unit_norm(lpad)
    loops[0].begin(mm3(halves, halves, 0, 0))
    norms = []
    for start, stop in ((0, low), (low, low + round_up(gr, 8))):
        value = spad[start:stop, :]
        total = jnp.sum(jnp.sum(value * value, axis=0, keepdims=True), axis=1, keepdims=True)
        norms.append(1.0 / (jnp.sqrt(total) + TINY))
    row = lax.broadcasted_iota(jnp.int32, (spad.shape[0], 1), 0)
    spad[...] = spad[...] * jnp.where(row < low, norms[0], norms[1])
    halves = split(spad[...])
    gram = mm3(halves, halves, 1, 1)
    i, j = (lax.broadcasted_iota(jnp.int32, gram.shape, d) for d in (0, 1))
    loops[1].begin(jnp.where((i < low) == (j < low), gram, 0.0))
    for k in (2, 3):
        loads[k].wait()
        stores[k].start()

    def light(k, carry):
        loops[0].light_step(k, carry)
        loops[1].step(k, carry)
        return carry

    def full(k, carry):
        for loop in loops:
            loop.step(k, carry)
        return carry

    lax.fori_loop(0, 2, light, 0)
    lax.fori_loop(2, 4, full, 0)
    prods = [loop.finish() for loop in loops]
    ortho = mm3(split(lpad[...]), prods[0], 1, 0)
    loads[1].wait()
    wl[...] = wl[...] - MUON_RATE * ortho[0:cat, 0:trans]
    stores[1].start()
    ortho = mm3(prods[1], split(spad[...]), 1, 0)
    wf_new[...] = wf[...] - MUON_RATE * ortho[0:bot, 0:c0]
    wg_new[...] = wg[...] - MUON_RATE * ortho[low : low + gr, 0 : 9 * bot]
    for copy in stores:
        copy.wait()


def per_device(counts, inputs, small_flags, norm_params, norm_moment, w_bottleneck, w_growth, w_transition,
               m_bottleneck, m_growth, m_transition, cotangent):
    rows, batch = counts
    images, band, width, c0 = inputs.shape
    bot, gr, trans = w_bottleneck.shape[1], w_growth.shape[1], w_transition.shape[1]
    own = cotangent.shape[0]
    cat = c0 + gr
    n_pix, n_cell = images * 64, images * 16
    assert rows == 4 and band == 4 and width == 16 and images % 16 == 0
    any_spec = pl.BlockSpec(memory_space=pl.ANY)
    vmem_spec = pl.BlockSpec(memory_space=pltpu.VMEM)
    smem_spec = pl.BlockSpec(memory_space=pltpu.SMEM)
    wide = round_up(c0, LANES)
    unit = 16 * 4 * batch
    blocks = -(-trans // LANES)
    rows_b = -(-c0 // LANES) * round_up(bot, 8)
    rows_c = (blocks + -(-9 * bot // LANES)) * round_up(gr, 8)
    length_a = round_up(blocks * round_up(c0, 16), unit)
    length_c = round_up(rows_b + rows_c, unit)
    dims = (rows, batch, images, c0, bot, gr, trans, own)
    v = pltpu.VMEM
    dma = pltpu.SemaphoreType.DMA

    def vector_scratch(height):
        return [v((rows, height, LANES), F32), v((batch, height, LANES), F32), dma((2, rows)), dma((2, batch))]

    scratch = [
        v((n_pix, c0), BF16), v((n_pix, c0), BF16), v((n_pix, c0), BF16),
        v((n_pix, LANES), F32), v((n_cell, LANES), F32),
        v((n_cell, c0), F32), v((n_cell, c0), BF16), v((n_cell, LANES), BF16),
        v((n_cell, wide), F32), v((n_cell, LANES), F32), v((images, 16, trans), BF16),
        v((images, 4, 16, bot), F32),
        v((images, 6, 16, bot), BF16), v((n_pix, bot), BF16), v((n_pix, LANES), F32),
        v((images, 6, 16, LANES), BF16), v((n_pix, bot), F32),
        v((cat, trans), F32), v((cat, trans), BF16), v((LANES, trans), BF16),
        v((bot, c0), F32), v((bot, c0), BF16), v((c0, bot), BF16), v((gr, 9 * bot), F32),
        v((4, 3 * LANES, bot), F32), v((3, bot, 3 * LANES), BF16), v((3 * LANES, bot), BF16),
        v((TILE_IMGS * 16, TILE_IMGS * 64), BF16), v((TILE_IMGS * 64, TILE_IMGS * 16), BF16),
        v((8, wide), F32), v((8, LANES), F32), v((n_cell, LANES), F32),
        dma((images // TILE_IMGS,)), dma((5,)), dma((2, rows)), dma((2, 2)), dma((2, 2)), dma((2, rows)),
    ]
    for height in (16, 8, 8, 8):
        scratch += vector_scratch(height)
    scratch += [dma((2, rows)), dma((2, batch))] + vector_scratch(16)
    for length in (length_a, length_c):
        scratch += BlockReduce.scratch(length, batch)
    scratch += [v((wide // LANES, 32, LANES), F32)]
    scratch += [v((images, 16, trans), BF16)]
    struct = jax.ShapeDtypeStruct
    input_grad, pooled, stats, sum_a, sum_c = pl.pallas_call(
        functools.partial(band_kernel, dims),
        out_shape=(
            struct((n_pix, c0), BF16),
            struct((own, 64, trans), BF16),
            struct((16, wide), F32),
            struct((length_a, LANES), BF16),
            struct((length_c, LANES), BF16),
        ),
        in_specs=[smem_spec, any_spec, any_spec, vmem_spec, any_spec, any_spec, any_spec],
        out_specs=[any_spec, any_spec, vmem_spec, any_spec, any_spec],
        scratch_shapes=scratch,
        compiler_params=pltpu.CompilerParams(collective_id=0, has_side_effects=True, vmem_limit_bytes=VMEM_BYTES),
        name="band",
    )(
        small_flags,
        inputs.reshape(n_pix, c0),
        cotangent.reshape(own, 64, trans),
        norm_params,
        w_bottleneck.T,
        w_growth.T,
        w_transition,
    )
    vectors = [struct(norm_params.shape, F32)] * 2
    weights = [struct((bot, c0), F32), struct((gr, 9 * bot), F32)]
    outs = pl.pallas_call(
        functools.partial(update_kernel, (c0, bot, gr, trans)),
        out_shape=[struct((n_pix, c0), BF16), struct((own, 64, trans), BF16)]
        + [struct((cat, trans), F32)] * 2
        + vectors
        + weights * 2,
        in_specs=[any_spec] * 4 + [vmem_spec] * 9,
        out_specs=[any_spec] * 4 + [vmem_spec] * 6,
        scratch_shapes=[
            v((round_up(cat, 128), 4 * LANES), F32),
            v((round_up(bot + gr + 16, 256), round_up(max(c0, 9 * bot), LANES)), F32),
            v((n_pix, c0), BF16),
            v((own, 64, trans), BF16),
            v((cat, trans), F32),
            v((cat, trans), F32),
            dma((2, 4)),
        ]
        + LoopedOrthogonal.scratch(4 * LANES)
        + LoopedOrthogonal.scratch(round_up(bot + gr + 16, 256)),
        compiler_params=pltpu.CompilerParams(vmem_limit_bytes=VMEM_BYTES),
        name="update",
    )(
        input_grad, pooled, w_transition, m_transition, stats, sum_a, sum_c, norm_params, norm_moment, w_bottleneck.T,
        w_growth.T, m_bottleneck.T, m_growth.T,
    )
    (ig, pooled, wl_new, ml_new, moment_new, params_new, mf_new, mg_new, wf_new, wg_new) = outs
    return (
        pooled.reshape(cotangent.shape),
        ig.reshape(inputs.shape),
        moment_new,
        params_new,
        mf_new.T,
        mg_new.T,
        ml_new,
        wf_new.T,
        wg_new.T,
        wl_new,
    )


def solution(mesh):
    counts = (mesh.shape["rows"], mesh.shape["batch"])
    whole = (P(),) * 8
    images = P(("batch", "rows"), None, None, None)
    bands = P("batch", "rows", None, None)
    return jax.shard_map(
        functools.partial(per_device, counts),
        mesh=mesh,
        in_specs=(bands, P("batch")) + whole + (images,),
        out_specs=(images, bands) + whole,
        check_vma=False,
    )
```
